512 devices in a mesh: blk: 64 (over y, z_lo, core), tgt: 8 (over x, z_hi).
Axes of the slice: x: 4, y: 4, z: 16 (z_hi: 2, z_lo: 8; z = z_hi * 8 + z_lo), core: 2. Of those that a mesh axis runs over, the one named last changes fastest.
Arguments:
- history: float32 [32768, 1536], P(('blk', 'tgt')), may hold values from 0 to 2
- weights: bfloat16 [64, 512, 32768], P(None, 'tgt', 'blk'), may hold values from -0.03125 to 0.03125
- delays: int32 [32, 32], replicated, may hold values from 16 to 64
- area_blocks: int32 [32], replicated, may hold values from 1 to 3, 64 in all
- potential: float32 [24, 32768], P(None, ('blk', 'tgt')), may hold values from -6 to 6
- leak: float32 [32768], P(('blk', 'tgt')), may hold values from 0.03 to 0.6
- drive: float32 [32768], P(('blk', 'tgt')), may hold values from -6 to 6
Outputs:
- rate_steps: float32 [16, 24, 32768], P(None, None, ('blk', 'tgt'))
- last_potential: float32 [24, 32768], P(None, ('blk', 'tgt'))
The draws below stay inside these ranges and needn't reach their ends.
Inputs may be any that keep to these rules, and one draw needn't show every extreme that they name: Area a consists of area_blocks[a] consecutive blocks of 512 neurons; areas follow one another in order.
All inputs are finite; a program needn't handle non-finite values.
Results may differ from the reference program's by a relative error of at most 0.00083.
Values may be sent and summed in bfloat16 or wider, within the bound.
A program may use at most 128 MiB of HBM per device.

```python
import math
import jax
import jax.numpy as jnp
import numpy as np
from jax import lax

NEURONS = 32768
TRIAL_TOTAL = 24
STEPS = 16
HIST = 64
AREAS = 32
BLOCK = 512
N_BLK = 64


def place_ends(values, own_key, smallest, largest):
    extent = values.shape
    index_at = [jax.random.randint(jax.random.fold_in(own_key, axis), (), 0, extent[axis]) for axis in range(len(extent))]
    values = values.at[tuple(index_at)].set(smallest)
    longest = extent.index(max(extent))
    index_at[longest] = (index_at[longest] + 1) % extent[longest]
    return values.at[tuple(index_at)].set(largest)


def block_levels(key, shape, split, low, largest):
    factor_of = 1.0
    for axis_at, parts in split:
        draws = jax.random.uniform(jax.random.fold_in(jax.random.fold_in(key, 6), axis_at), (parts,), jnp.float32, low / len(split), largest / len(split))
        factor_of = factor_of * jnp.repeat(jnp.exp(draws), shape[axis_at] // parts).reshape((-1,) + (1,) * (len(shape) - 1 - axis_at))
    return factor_of


def length_profile(count, total, bound, skew):
    portions = [(1 << 20) // math.isqrt(rank ** skew) + 1 for rank in range(2, count + 1)]
    rest, counts = total - bound - (count - 1), [1] * (count - 1)
    while rest > 0:
        candidates = [i for i in range(count - 1) if counts[i] < bound]
        mass, left = sum([portions[i] for i in candidates]), rest
        for i in candidates:
            addition = min(bound - counts[i], max(1, left * portions[i] // mass), rest)
            counts[i] = counts[i] + addition
            rest = rest - addition
    return np.array([bound] + counts)


def ragged_sizes(key, number_of, total, limit, slope):
    if number_of == 2:
        one = jax.random.randint(key, (), max(1, total - limit), min(limit, total - 1) + 1)
        return jnp.stack([one, total - one])
    lengths = jnp.asarray(length_profile(number_of, total, limit, slope), jnp.int32)
    twos = (number_of - 1) // 2
    source_of, receiver = lengths[1:1 + 2 * twos:2], lengths[2:2 + 2 * twos:2]
    slack = jnp.minimum(source_of - 1, limit - receiver)
    moved = jax.random.randint(jax.random.fold_in(key, 1), (twos,), 0, 1 << 20) % (slack + 1)
    lengths = lengths.at[1:1 + 2 * twos:2].set(source_of - moved).at[2:2 + 2 * twos:2].set(receiver + moved)
    return lengths[jax.random.permutation(jax.random.fold_in(key, 2), number_of)]


def scatter_about(stream_key, extent, spread, limit, split=(), held_as=jnp.bfloat16):
    array = spread * jax.random.normal(stream_key, extent, jnp.float32)
    if split:
        array = array * block_levels(stream_key, extent, split, -0.22, 0.18)
    return jnp.clip(array, -limit, limit).astype(held_as)


def setup_inputs(seed: int = 0) -> dict:
    key_list = jax.random.split(jax.random.key(seed), 8)
    return {
        "history": jnp.clip(2.0 * jax.random.uniform(key_list[0], (NEURONS, HIST * TRIAL_TOTAL), jnp.float32) ** block_levels(key_list[0], (NEURONS, HIST * TRIAL_TOTAL), ((0, 512),), -0.2, 0.2), 0.0, 2.0),
        "weights": scatter_about(key_list[1], (N_BLK, BLOCK, NEURONS), NEURONS ** -0.5, 0.03125, ((1, 8), (2, 64))),
        "delays": place_ends(jax.random.randint(key_list[2], (AREAS, AREAS), 16, 65), jax.random.fold_in(key_list[2], 1), 16, 64).astype(jnp.int32),
        "area_blocks": ragged_sizes(key_list[3], AREAS, N_BLK, 3, 1).astype(jnp.int32),
        "potential": scatter_about(key_list[4], (TRIAL_TOTAL, NEURONS), 1.0, 6.0, ((1, 512),), jnp.float32),
        "leak": jnp.clip(jnp.exp(math.log(0.6) - 2.9957323 * jax.random.uniform(key_list[5], (NEURONS,), jnp.float32) ** block_levels(key_list[5], (NEURONS,), ((0, 512),), -0.2, 0.2)), 0.03, 0.6),
        "drive": scatter_about(key_list[6], (NEURONS,), 1.0, 6.0, ((0, 512),), jnp.float32),
    }


def block_areas(area_blocks, block_count):
    boundary = jnp.cumsum(area_blocks)
    blocks = jnp.arange(block_count, dtype=jnp.int32)
    return jnp.sum((boundary[None, :] <= blocks[:, None]).astype(jnp.int32), axis=1)


def reference(history, weights, delays, area_blocks, potential, leak, drive):
    area_of_block = block_areas(area_blocks, N_BLK)
    history_low = history.astype(jnp.bfloat16).reshape(N_BLK, BLOCK, HIST * TRIAL_TOTAL)

    def window(lag_step, column):
        start = ((HIST - lag_step) * TRIAL_TOTAL).astype(jnp.int32)
        return lax.dynamic_slice_in_dim(column, start, STEPS * TRIAL_TOTAL, 1)

    def one_target(target_block):
        lag_steps = delays[area_of_block[target_block]][area_of_block]
        delayed_input = jax.vmap(window, in_axes=(0, 0))(lag_steps, history_low)
        weight_column_slice = lax.dynamic_slice_in_dim(weights, (target_block * BLOCK).astype(jnp.int32), BLOCK, 2)
        return jnp.einsum("gyw,gyt->wt", delayed_input.astype(jnp.float32), weight_column_slice.astype(jnp.float32))

    inputs = lax.map(one_target, jnp.arange(N_BLK, dtype=jnp.int32))
    inputs = inputs.transpose(1, 0, 2).reshape(STEPS, TRIAL_TOTAL, NEURONS)

    def advance(membrane_state, synaptic):
        membrane_state = membrane_state + leak * (drive - membrane_state + synaptic)
        return membrane_state, jax.nn.softplus(membrane_state)

    last_potential, rate_steps = lax.scan(advance, potential, inputs)
    return rate_steps, last_potential
```

```python
import functools

import jax
import jax.numpy as jnp
from jax import lax
from jax.experimental import pallas as pl
from jax.experimental.pallas import tpu as pltpu
from jax.sharding import PartitionSpec as P

MESH = pl.DeviceIdType.MESH
STEPS = 16
TRIALS = 24
GROUP = 8
PASSES = TRIALS // GROUP
HIST = 64
SPANS = HIST // STEPS
SHARE = 64
CHAIN = 8
RING = 4
PEERS = 8
AREAS = 32
LANES = STEPS * GROUP
OFFSET = 3
LAG = 3


def kernel(
    hist_ref, weights_hbm, delays_ref, blocks_ref, pot_ref, leak_ref, drive_ref,
    rates_ref, last_ref,
    weights, hbuf, spans, sent, got, acc, xgot, zsend, zgot, src_area, tgt_area,
    w_sem, zsend_sem, zrecv_sem, ysend_sem, yrecv_sem, xsend_sem, xrecv_sem, hsend_sem, hrecv_sem,
):
    blk = lax.axis_index("blk")
    tgt = lax.axis_index("tgt")
    core = lax.rem(blk, 2)
    z = lax.rem(blk // 2, CHAIN)
    y = blk // (2 * CHAIN)
    x = tgt // 2
    z_hi = lax.rem(tgt, 2)

    def block_at(yy, zz, cc):
        return (yy * CHAIN + zz) * 2 + cc

    def peer_block(k, zz):
        dy, dc = k // 2, k % 2
        return block_at(lax.rem(y + dy, RING), zz, lax.rem(core + dc, 2))

    def x_peer(dx):
        return (blk, lax.rem(x + dx, RING) * 2 + z_hi)

    across = (blk, x * 2 + 1 - z_hi)
    right = (block_at(y, z + 1, core), tgt)
    left = (block_at(y, z - 1, core), tgt)

    barrier = pltpu.get_barrier_semaphore()
    for k in range(1, PEERS):
        pl.semaphore_signal(barrier, 1, device_id=(peer_block(k, z), tgt), device_id_type=MESH)
    for dx in range(1, RING):
        pl.semaphore_signal(barrier, 1, device_id=x_peer(dx), device_id_type=MESH)
    pl.semaphore_signal(barrier, 1, device_id=across, device_id_type=MESH)

    @pl.when(z < CHAIN - 1)
    def _():
        pl.semaphore_signal(barrier, 1, device_id=right, device_id_type=MESH)

    @pl.when(z > 0)
    def _():
        pl.semaphore_signal(barrier, 1, device_id=left, device_id_type=MESH)

    w_copy = pltpu.make_async_copy(weights_hbm, weights, w_sem)
    w_copy.start()

    width = STEPS * TRIALS
    row = lax.broadcasted_iota(jnp.int32, (width, width), 0)
    col = lax.broadcasted_iota(jnp.int32, (width, width), 1)
    inner = lax.rem(col, LANES)
    wanted = (inner // GROUP) * TRIALS + (col // LANES) * GROUP + lax.rem(inner, GROUP)
    regroup = jnp.where(row == wanted, 1.0, 0.0).astype(jnp.bfloat16)
    for q in range(SPANS):
        part = hist_ref[:, q * width : (q + 1) * width].astype(jnp.bfloat16)
        moved = jnp.dot(part, regroup, preferred_element_type=jnp.float32).astype(jnp.bfloat16)
        for c in range(PASSES):
            hbuf[c, 0, q] = moved[:, c * LANES : (c + 1) * LANES]
    acc[...] = jnp.zeros_like(acc)

    sources = [block_at(y, zz, core) for zz in range(CHAIN)]
    targets = [peer_block(k, z) for k in range(PEERS)]

    def count(a, carry):
        edge, counts = carry[0] + blocks_ref[a], carry[1:]
        more = [n + jnp.where(edge <= b, 1, 0) for n, b in zip(counts, sources + targets)]
        return (edge, *more)

    counted = lax.fori_loop(0, AREAS, count, (jnp.int32(0),) * (1 + CHAIN + PEERS))[1:]
    for i in range(CHAIN):
        src_area[i] = jnp.minimum(counted[i], AREAS - 1)
    for i in range(PEERS):
        tgt_area[i] = jnp.minimum(counted[CHAIN + i], AREAS - 1)

    pl.semaphore_wait(
        barrier, PEERS - 1 + RING - 1 + 1 + jnp.where(z < CHAIN - 1, 1, 0) + jnp.where(z > 0, 1, 0)
    )

    def source_of(t):
        both = jnp.minimum(z, CHAIN - 1 - z)
        dist = jnp.where(t <= 2 * both, (t + 1) // 2, t - both)
        from_left = jnp.where(t <= 2 * both, lax.rem(t, 2), jnp.where(z >= CHAIN // 2, 1, 0))
        return jnp.where(from_left == 1, z - dist, z + dist)

    def slot_at(zr, zs):
        both = jnp.minimum(zr, CHAIN - 1 - zr)
        dist = jnp.abs(zr - zs)
        return jnp.where(dist <= both, 2 * dist - jnp.where(zs < zr, 1, 0), dist + both)

    def chain_copy(c, t, zs, to_right):
        there = slot_at(z + 1 if to_right else z - 1, zs)
        return pltpu.make_async_remote_copy(
            src_ref=hbuf.at[c, t],
            dst_ref=hbuf.at[c, there],
            send_sem=zsend_sem.at[1 if to_right else 0, c, t],
            recv_sem=zrecv_sem.at[c, there],
            device_id=right if to_right else left,
            device_id_type=MESH,
        )

    def chain_arrival(c, t):
        return pltpu.make_async_remote_copy(
            src_ref=hbuf.at[c, t],
            dst_ref=hbuf.at[c, t],
            send_sem=zsend_sem.at[0, c, t],
            recv_sem=zrecv_sem.at[c, t],
            device_id=left,
            device_id_type=MESH,
        )

    def goes_right(zs):
        return jnp.logical_and(zs <= z, z < CHAIN - 1)

    def goes_left(zs):
        return jnp.logical_and(zs >= z, z > 0)

    lane = lax.broadcasted_iota(jnp.int32, (SHARE, LANES), 1)

    def spread(c, t):
        @pl.when(t > 0)
        def _():
            chain_arrival(c, t).wait_recv()

        zs = source_of(t)

        @pl.when(goes_right(zs))
        def _():
            chain_copy(c, t, zs, True).start()

        @pl.when(goes_left(zs))
        def _():
            chain_copy(c, t, zs, False).start()

        for q in range(SPANS):
            spans[q] = hbuf[c, t, q].astype(jnp.float32)
        area = src_area[zs]
        for k in [1, 2, 3, 6, 7, 4, 5, 0]:
            begin = jnp.clip(HIST - delays_ref[tgt_area[k], area], 0, HIST - STEPS)
            span = begin // STEPS
            skip = lax.rem(begin, STEPS) * GROUP
            turn = lax.rem(LANES - skip, LANES)
            first = pltpu.roll(spans[span], turn, 1)
            second = pltpu.roll(spans[jnp.minimum(span + 1, SPANS - 1)], turn, 1)
            window = jnp.where(lane < LANES - skip, first, second).astype(jnp.bfloat16)
            if k == 0:
                got[c, t, 0] = window
            else:
                sent[c, t, k - 1] = window
                back = (RING - k // 2) % RING * 2 + k % 2
                pltpu.make_async_remote_copy(
                    src_ref=sent.at[c, t, k - 1],
                    dst_ref=got.at[c, t, back],
                    send_sem=ysend_sem.at[c, t],
                    recv_sem=yrecv_sem.at[c, t],
                    device_id=(peer_block(k, z), tgt),
                    device_id_type=MESH,
                ).start()

    def windows_copy(c, t):
        return pltpu.make_async_remote_copy(
            src_ref=sent.at[c, t],
            dst_ref=got.at[c, t, pl.ds(1, PEERS - 1)],
            send_sem=ysend_sem.at[c, t],
            recv_sem=yrecv_sem.at[c, t],
            device_id=(peer_block(1, z), tgt),
            device_id_type=MESH,
        )

    def product(c, t):
        windows_copy(c, t).wait_recv()
        zs = source_of(t)
        rows = got[c, t].reshape(PEERS * SHARE, LANES)
        columns = jnp.concatenate([weights[peer_block(k, zs)] for k in range(PEERS)], axis=0)
        sums = lax.dot_general(
            rows, columns, (((0,), (0,)), ((), ())), preferred_element_type=jnp.float32
        )
        for i in range(RING):
            acc[c, i] += sums[:, i * 2 * SHARE : (i + 1) * 2 * SHARE]

    def x_copy(c, dx):
        return pltpu.make_async_remote_copy(
            src_ref=acc.at[c, lax.rem(x + dx, RING)],
            dst_ref=xgot.at[c, RING - 1 - dx],
            send_sem=xsend_sem.at[c],
            recv_sem=xrecv_sem.at[c],
            device_id=x_peer(dx),
            device_id_type=MESH,
        )

    def x_all(c):
        return pltpu.make_async_remote_copy(
            src_ref=acc.at[c, pl.ds(0, RING - 1)],
            dst_ref=xgot.at[c],
            send_sem=xsend_sem.at[c],
            recv_sem=xrecv_sem.at[c],
            device_id=x_peer(1),
            device_id_type=MESH,
        )

    def z_copy(c):
        return pltpu.make_async_remote_copy(
            src_ref=zsend.at[c, 0],
            dst_ref=zgot.at[c],
            send_sem=hsend_sem.at[c],
            recv_sem=hrecv_sem.at[c],
            device_id=across,
            device_id_type=MESH,
        )

    def sum_x(c):
        x_all(c).wait_recv()
        total = acc[c, x] + xgot[c, 0] + xgot[c, 1] + xgot[c, 2]
        early, late = total[: LANES // 2], total[LANES // 2 :]
        share0 = jnp.where(lane < SHARE, early, pltpu.roll(late, SHARE, 1))
        share1 = jnp.where(lane < SHARE, pltpu.roll(early, SHARE, 1), late)
        zsend[c, z_hi] = share1
        zsend[c, 1 - z_hi] = share0
        z_copy(c).start()

    def integrate(c):
        z_copy(c).wait_recv()
        total = zsend[c, 1] + zgot[c]
        turned = pltpu.roll(total, SHARE, 1)
        mine = pl.ds(pl.multiple_of(c * GROUP, GROUP), GROUP)
        membrane = pot_ref[mine, :]
        leak, drive = leak_ref[...], drive_ref[...]
        for s in range(STEPS):
            half = total if s < STEPS // 2 else turned
            begin = s % (STEPS // 2) * GROUP
            synaptic = half[begin : begin + GROUP, :SHARE]
            membrane = membrane + leak * (drive - membrane + synaptic)
            rates_ref[s, mine, :] = jnp.maximum(membrane, 0.0) + jnp.log1p(jnp.exp(-jnp.abs(membrane)))
        last_ref[mine, :] = membrane

    w_copy.wait()

    def slot(k, _):
        def one(c, _):
            t = k - OFFSET * c

            @pl.when(jnp.logical_and(t >= 0, t < CHAIN))
            def _():
                spread(c, t)

            return 0

        def two(c, _):
            t = k - OFFSET * c - LAG

            @pl.when(jnp.logical_and(t >= 0, t < CHAIN))
            def _():
                product(c, t)

            @pl.when(t == CHAIN - 1)
            def _():
                for dx in range(1, RING):
                    x_copy(c, dx).start()

            return 0

        def three(c, _):
            t = k - OFFSET * c - LAG

            @pl.when(t == CHAIN)
            def _():
                sum_x(c)

            @pl.when(t == CHAIN + 1)
            def _():
                integrate(c)

            return 0

        lax.fori_loop(0, PASSES, one, 0)
        lax.fori_loop(0, PASSES, three, 0)
        lax.fori_loop(0, PASSES, two, 0)
        return 0

    lax.fori_loop(0, OFFSET * (PASSES - 1) + CHAIN + LAG + 2, slot, 0)

    def drain(n, _):
        c, t = n // CHAIN, lax.rem(n, CHAIN)
        zs = source_of(t)

        @pl.when(goes_right(zs))
        def _():
            chain_copy(c, t, zs, True).wait_send()

        @pl.when(goes_left(zs))
        def _():
            chain_copy(c, t, zs, False).wait_send()

        windows_copy(c, t).wait_send()

        @pl.when(t == 0)
        def _():
            x_all(c).wait_send()
            z_copy(c).wait_send()

        return 0

    lax.fori_loop(0, PASSES * CHAIN, drain, 0)


def on_device(history, weights, delays, area_blocks, potential, leak, drive):
    vmem = pl.BlockSpec(memory_space=pltpu.VMEM)
    smem = pl.BlockSpec(memory_space=pltpu.SMEM)
    dma = pltpu.SemaphoreType.DMA
    bf16, f32 = jnp.bfloat16, jnp.float32
    return pl.pallas_call(
        kernel,
        out_shape=(
            jax.ShapeDtypeStruct((STEPS, TRIALS, SHARE), f32),
            jax.ShapeDtypeStruct((TRIALS, SHARE), f32),
        ),
        in_specs=[vmem, pl.BlockSpec(memory_space=pl.ANY), smem, smem, vmem, vmem, vmem],
        out_specs=(vmem, vmem),
        scratch_shapes=[
            pltpu.VMEM(weights.shape, bf16),
            pltpu.VMEM((PASSES, CHAIN, SPANS, SHARE, LANES), bf16),
            pltpu.VMEM((SPANS, SHARE, LANES), f32),
            pltpu.VMEM((PASSES, CHAIN, PEERS - 1, SHARE, LANES), bf16),
            pltpu.VMEM((PASSES, CHAIN, PEERS, SHARE, LANES), bf16),
            pltpu.VMEM((PASSES, RING, LANES, 2 * SHARE), f32),
            pltpu.VMEM((PASSES, RING - 1, LANES, 2 * SHARE), f32),
            pltpu.VMEM((PASSES, 2, LANES // 2, 2 * SHARE), f32),
            pltpu.VMEM((PASSES, LANES // 2, 2 * SHARE), f32),
            pltpu.SMEM((CHAIN,), jnp.int32),
            pltpu.SMEM((PEERS,), jnp.int32),
            dma,
            dma((2, PASSES, CHAIN)),
            dma((PASSES, CHAIN)),
            dma((PASSES, CHAIN)),
            dma((PASSES, CHAIN)),
            dma((PASSES,)),
            dma((PASSES,)),
            dma((PASSES,)),
            dma((PASSES,)),
        ],
        compiler_params=pltpu.CompilerParams(
            collective_id=0, has_side_effects=True, vmem_limit_bytes=40 * 2**20
        ),
        name="network_interval",
    )(history, weights, delays, area_blocks, potential, leak.reshape(1, -1), drive.reshape(1, -1))


def solution(mesh):
    in_specs = (
        P(("blk", "tgt"), None),
        P(None, "tgt", "blk"),
        P(),
        P(),
        P(None, ("blk", "tgt")),
        P(("blk", "tgt")),
        P(("blk", "tgt")),
    )
    out_specs = (P(None, None, ("blk", "tgt")), P(None, ("blk", "tgt")))
    return jax.shard_map(
        on_device, mesh=mesh, in_specs=in_specs, out_specs=out_specs, check_vma=False
    )
```

```python
import functools

import jax
import jax.numpy as jnp
from jax import lax
from jax.experimental import pallas as pl
from jax.experimental.pallas import tpu as pltpu
from jax.sharding import PartitionSpec as P

MESH = pl.DeviceIdType.MESH
STEPS = 16
TRIALS = 24
GROUP = 8
PASSES = TRIALS // GROUP
HIST = 64
SPANS = HIST // STEPS
SHARE = 64
CHAIN = 8
RING = 4
PEERS = 8
AREAS = 32
LANES = STEPS * GROUP
OFFSET = 0
LAG = 2


def kernel(
    hist_hbm, weights_hbm, delays_hbm, blocks_hbm, pot_hbm, leak_hbm, drive_hbm,
    rates_ref, last_ref,
    hist_ref, weights, delays_ref, blocks_ref, pot_ref, leak_ref, drive_ref, hbuf, spans, sent, got, acc, xgot, zsend, zgot, src_area, tgt_area,
    in_sem, zsend_sem, zrecv_sem, ysend_sem, yrecv_sem, xsend_sem, xrecv_sem, hsend_sem, hrecv_sem,
):
    blk = lax.axis_index("blk")
    tgt = lax.axis_index("tgt")
    core = lax.rem(blk, 2)
    z = lax.rem(blk // 2, CHAIN)
    y = blk // (2 * CHAIN)
    x = tgt // 2
    z_hi = lax.rem(tgt, 2)

    def block_at(yy, zz, cc):
        return (yy * CHAIN + zz) * 2 + cc

    def peer_block(k, zz):
        dy, dc = k // 2, k % 2
        return block_at(lax.rem(y + dy, RING), zz, lax.rem(core + dc, 2))

    def x_peer(dx):
        return (blk, lax.rem(x + dx, RING) * 2 + z_hi)

    across = (blk, x * 2 + 1 - z_hi)
    right = (block_at(y, z + 1, core), tgt)
    left = (block_at(y, z - 1, core), tgt)

    pairs = [
        (hist_hbm, hist_ref), (blocks_hbm, blocks_ref), (delays_hbm, delays_ref), (weights_hbm, weights),
        (pot_hbm, pot_ref), (leak_hbm, leak_ref), (drive_hbm, drive_ref),
    ]
    loads = [pltpu.make_async_copy(a, b, in_sem.at[i]) for i, (a, b) in enumerate(pairs)]
    for load in loads:
        load.start()

    barrier = pltpu.get_barrier_semaphore()
    for k in range(1, PEERS):
        pl.semaphore_signal(barrier, 1, device_id=(peer_block(k, z), tgt), device_id_type=MESH)
    for dx in range(1, RING):
        pl.semaphore_signal(barrier, 1, device_id=x_peer(dx), device_id_type=MESH)
    pl.semaphore_signal(barrier, 1, device_id=across, device_id_type=MESH)

    @pl.when(z < CHAIN - 1)
    def _():
        pl.semaphore_signal(barrier, 1, device_id=right, device_id_type=MESH)

    @pl.when(z > 0)
    def _():
        pl.semaphore_signal(barrier, 1, device_id=left, device_id_type=MESH)

    width = STEPS * TRIALS
    row = lax.broadcasted_iota(jnp.int32, (width, width), 0)
    col = lax.broadcasted_iota(jnp.int32, (width, width), 1)
    inner = lax.rem(col, LANES)
    wanted = (inner // GROUP) * TRIALS + (col // LANES) * GROUP + lax.rem(inner, GROUP)
    regroup = jnp.where(row == wanted, 1.0, 0.0).astype(jnp.bfloat16)
    loads[0].wait()
    for q in range(SPANS):
        part = hist_ref[:, q * width : (q + 1) * width].astype(jnp.bfloat16)
        moved = jnp.dot(part, regroup, preferred_element_type=jnp.float32).astype(jnp.bfloat16)
        for c in range(PASSES):
            hbuf[c, 0, q] = moved[:, c * LANES : (c + 1) * LANES]
    acc[...] = jnp.zeros_like(acc)

    sources = [block_at(y, zz, core) for zz in range(CHAIN)]
    targets = [peer_block(k, z) for k in range(PEERS)]

    def count(a, carry):
        edge, counts = carry[0] + blocks_ref[a], carry[1:]
        more = [n + jnp.where(edge <= b, 1, 0) for n, b in zip(counts, sources + targets)]
        return (edge, *more)

    loads[1].wait()
    counted = lax.fori_loop(0, AREAS, count, (jnp.int32(0),) * (1 + CHAIN + PEERS))[1:]
    for i in range(CHAIN):
        src_area[i] = jnp.minimum(counted[i], AREAS - 1)
    for i in range(PEERS):
        tgt_area[i] = jnp.minimum(counted[CHAIN + i], AREAS - 1)

    pl.semaphore_wait(
        barrier, PEERS - 1 + RING - 1 + 1 + jnp.where(z < CHAIN - 1, 1, 0) + jnp.where(z > 0, 1, 0)
    )

    def source_of(t):
        both = jnp.minimum(z, CHAIN - 1 - z)
        dist = jnp.where(t <= 2 * both, (t + 1) // 2, t - both)
        from_left = jnp.where(t <= 2 * both, lax.rem(t, 2), jnp.where(z >= CHAIN // 2, 1, 0))
        return jnp.where(from_left == 1, z - dist, z + dist)

    def slot_at(zr, zs):
        both = jnp.minimum(zr, CHAIN - 1 - zr)
        dist = jnp.abs(zr - zs)
        return jnp.where(dist <= both, 2 * dist - jnp.where(zs < zr, 1, 0), dist + both)

    def chain_copy(c, t, zs, to_right):
        there = slot_at(z + 1 if to_right else z - 1, zs)
        return pltpu.make_async_remote_copy(
            src_ref=hbuf.at[c, t],
            dst_ref=hbuf.at[c, there],
            send_sem=zsend_sem.at[1 if to_right else 0, c, t],
            recv_sem=zrecv_sem.at[c, there],
            device_id=right if to_right else left,
            device_id_type=MESH,
        )

    def chain_arrival(c, t):
        return pltpu.make_async_remote_copy(
            src_ref=hbuf.at[c, t],
            dst_ref=hbuf.at[c, t],
            send_sem=zsend_sem.at[0, c, t],
            recv_sem=zrecv_sem.at[c, t],
            device_id=left,
            device_id_type=MESH,
        )

    def goes_right(zs):
        return jnp.logical_and(zs <= z, z < CHAIN - 1)

    def goes_left(zs):
        return jnp.logical_and(zs >= z, z > 0)

    lane = lax.broadcasted_iota(jnp.int32, (SHARE, LANES), 1)

    def spread(c, t):
        @pl.when(t > 0)
        def _():
            chain_arrival(c, t).wait_recv()

        zs = source_of(t)

        @pl.when(goes_right(zs))
        def _():
            chain_copy(c, t, zs, True).start()

        @pl.when(goes_left(zs))
        def _():
            chain_copy(c, t, zs, False).start()

        for q in range(SPANS):
            spans[q] = hbuf[c, t, q].astype(jnp.float32)
        area = src_area[zs]
        for k in [1, 2, 3, 6, 7, 4, 5, 0]:
            begin = jnp.clip(HIST - delays_ref[tgt_area[k], area], 0, HIST - STEPS)
            span = begin // STEPS
            skip = lax.rem(begin, STEPS) * GROUP
            turn = lax.rem(LANES - skip, LANES)
            first = pltpu.roll(spans[span], turn, 1)
            second = pltpu.roll(spans[jnp.minimum(span + 1, SPANS - 1)], turn, 1)
            window = jnp.where(lane < LANES - skip, first, second).astype(jnp.bfloat16)
            if k == 0:
                got[c, t, 0] = window
            else:
                sent[c, t, k - 1] = window
                back = (RING - k // 2) % RING * 2 + k % 2
                pltpu.make_async_remote_copy(
                    src_ref=sent.at[c, t, k - 1],
                    dst_ref=got.at[c, t, back],
                    send_sem=ysend_sem.at[c, t],
                    recv_sem=yrecv_sem.at[c, t],
                    device_id=(peer_block(k, z), tgt),
                    device_id_type=MESH,
                ).start()

    def windows_copy(c, t):
        return pltpu.make_async_remote_copy(
            src_ref=sent.at[c, t],
            dst_ref=got.at[c, t, pl.ds(1, PEERS - 1)],
            send_sem=ysend_sem.at[c, t],
            recv_sem=yrecv_sem.at[c, t],
            device_id=(peer_block(1, z), tgt),
            device_id_type=MESH,
        )

    def product(c, t):
        windows_copy(c, t).wait_recv()
        zs = source_of(t)
        rows = got[c, t].reshape(PEERS * SHARE, LANES)
        columns = jnp.concatenate([weights[peer_block(k, zs)] for k in range(PEERS)], axis=0)
        sums = lax.dot_general(
            rows, columns, (((0,), (0,)), ((), ())), preferred_element_type=jnp.float32
        )
        for i in range(RING):
            acc[c, i] += sums[:, i * 2 * SHARE : (i + 1) * 2 * SHARE]

    def x_copy(c, dx):
        return pltpu.make_async_remote_copy(
            src_ref=acc.at[c, lax.rem(x + dx, RING)],
            dst_ref=xgot.at[c, RING - 1 - dx],
            send_sem=xsend_sem.at[c],
            recv_sem=xrecv_sem.at[c],
            device_id=x_peer(dx),
            device_id_type=MESH,
        )

    def x_all(c):
        return pltpu.make_async_remote_copy(
            src_ref=acc.at[c, pl.ds(0, RING - 1)],
            dst_ref=xgot.at[c],
            send_sem=xsend_sem.at[c],
            recv_sem=xrecv_sem.at[c],
            device_id=x_peer(1),
            device_id_type=MESH,
        )

    def z_copy(c):
        return pltpu.make_async_remote_copy(
            src_ref=zsend.at[c, 0],
            dst_ref=zgot.at[c],
            send_sem=hsend_sem.at[c],
            recv_sem=hrecv_sem.at[c],
            device_id=across,
            device_id_type=MESH,
        )

    def sum_x(c):
        x_all(c).wait_recv()
        total = acc[c, x] + xgot[c, 0] + xgot[c, 1] + xgot[c, 2]
        early, late = total[: LANES // 2], total[LANES // 2 :]
        share0 = jnp.where(lane < SHARE, early, pltpu.roll(late, SHARE, 1))
        share1 = jnp.where(lane < SHARE, pltpu.roll(early, SHARE, 1), late)
        zsend[c, z_hi] = share1
        zsend[c, 1 - z_hi] = share0
        z_copy(c).start()

    def integrate(c):
        z_copy(c).wait_recv()
        total = zsend[c, 1] + zgot[c]
        turned = pltpu.roll(total, SHARE, 1)
        mine = pl.ds(pl.multiple_of(c * GROUP, GROUP), GROUP)
        membrane = pot_ref[mine, :]
        leak, drive = leak_ref[...], drive_ref[...]
        for s in range(STEPS):
            half = total if s < STEPS // 2 else turned
            begin = s % (STEPS // 2) * GROUP
            synaptic = half[begin : begin + GROUP, :SHARE]
            membrane = membrane + leak * (drive - membrane + synaptic)
            rates_ref[s, mine, :] = jnp.maximum(membrane, 0.0) + jnp.log1p(jnp.exp(-jnp.abs(membrane)))
        last_ref[mine, :] = membrane

    for load in loads[2:]:
        load.wait()

    def slot(k, _):
        def one(c, _):
            t = k - OFFSET * c

            @pl.when(jnp.logical_and(t >= 0, t < CHAIN))
            def _():
                spread(c, t)

            return 0

        def two(c, _):
            t = k - OFFSET * c - LAG

            @pl.when(jnp.logical_and(t >= 0, t < CHAIN))
            def _():
                product(c, t)

            @pl.when(t == CHAIN - 1)
            def _():
                for dx in range(1, RING):
                    x_copy(c, dx).start()

            return 0

        def three(c, _):
            t = k - OFFSET * c - LAG

            @pl.when(t == CHAIN)
            def _():
                sum_x(c)

            @pl.when(t == CHAIN + 1)
            def _():
                integrate(c)

            return 0

        lax.fori_loop(0, PASSES, one, 0)
        lax.fori_loop(0, PASSES, three, 0)
        lax.fori_loop(0, PASSES, two, 0)
        return 0

    lax.fori_loop(0, OFFSET * (PASSES - 1) + CHAIN + LAG + 2, slot, 0)

    def drain(n, _):
        c, t = n // CHAIN, lax.rem(n, CHAIN)
        zs = source_of(t)

        @pl.when(goes_right(zs))
        def _():
            chain_copy(c, t, zs, True).wait_send()

        @pl.when(goes_left(zs))
        def _():
            chain_copy(c, t, zs, False).wait_send()

        windows_copy(c, t).wait_send()

        @pl.when(t == 0)
        def _():
            x_all(c).wait_send()
            z_copy(c).wait_send()

        return 0

    lax.fori_loop(0, PASSES * CHAIN, drain, 0)


def on_device(history, weights, delays, area_blocks, potential, leak, drive):
    vmem = pl.BlockSpec(memory_space=pltpu.VMEM)
    dma = pltpu.SemaphoreType.DMA
    bf16, f32 = jnp.bfloat16, jnp.float32
    return pl.pallas_call(
        kernel,
        out_shape=(
            jax.ShapeDtypeStruct((STEPS, TRIALS, SHARE), f32),
            jax.ShapeDtypeStruct((TRIALS, SHARE), f32),
        ),
        in_specs=[pl.BlockSpec(memory_space=pltpu.HBM)] * 7,
        out_specs=(vmem, vmem),
        scratch_shapes=[
            pltpu.VMEM(history.shape, f32),
            pltpu.VMEM(weights.shape, bf16),
            pltpu.SMEM(delays.shape, jnp.int32),
            pltpu.SMEM(area_blocks.shape, jnp.int32),
            pltpu.VMEM(potential.shape, f32),
            pltpu.VMEM((1, SHARE), f32),
            pltpu.VMEM((1, SHARE), f32),
            pltpu.VMEM((PASSES, CHAIN, SPANS, SHARE, LANES), bf16),
            pltpu.VMEM((SPANS, SHARE, LANES), f32),
            pltpu.VMEM((PASSES, CHAIN, PEERS - 1, SHARE, LANES), bf16),
            pltpu.VMEM((PASSES, CHAIN, PEERS, SHARE, LANES), bf16),
            pltpu.VMEM((PASSES, RING, LANES, 2 * SHARE), f32),
            pltpu.VMEM((PASSES, RING - 1, LANES, 2 * SHARE), f32),
            pltpu.VMEM((PASSES, 2, LANES // 2, 2 * SHARE), f32),
            pltpu.VMEM((PASSES, LANES // 2, 2 * SHARE), f32),
            pltpu.SMEM((CHAIN,), jnp.int32),
            pltpu.SMEM((PEERS,), jnp.int32),
            dma((7,)),
            dma((2, PASSES, CHAIN)),
            dma((PASSES, CHAIN)),
            dma((PASSES, CHAIN)),
            dma((PASSES, CHAIN)),
            dma((PASSES,)),
            dma((PASSES,)),
            dma((PASSES,)),
            dma((PASSES,)),
        ],
        compiler_params=pltpu.CompilerParams(
            collective_id=0, has_side_effects=True, vmem_limit_bytes=56 * 2**20
        ),
        name="network_interval",
    )(history, weights, delays, area_blocks, potential, leak.reshape(1, -1), drive.reshape(1, -1))


def solution(mesh):
    in_specs = (
        P(("blk", "tgt"), None),
        P(None, "tgt", "blk"),
        P(),
        P(),
        P(None, ("blk", "tgt")),
        P(("blk", "tgt")),
        P(("blk", "tgt")),
    )
    out_specs = (P(None, None, ("blk", "tgt")), P(None, ("blk", "tgt")))
    return jax.shard_map(
        on_device, mesh=mesh, in_specs=in_specs, out_specs=out_specs, check_vma=False
    )
```

```python
import functools

import jax
import jax.numpy as jnp
from jax import lax
from jax.experimental import pallas as pl
from jax.experimental.pallas import tpu as pltpu
from jax.sharding import PartitionSpec as P

MESH = pl.DeviceIdType.MESH
STEPS = 16
TRIALS = 24
GROUP = 8
PASSES = TRIALS // GROUP
HIST = 64
SPANS = HIST // STEPS
SHARE = 64
CHAIN = 8
RING = 4
PEERS = 8
AREAS = 32
LANES = STEPS * GROUP
OFFSET = 0
SPAN_TYPE = jnp.bfloat16
ORDER = (4, 5, 2, 3, 6, 7, 1, 0)

LAG = 3


def kernel(
    hist_hbm, weights_hbm, delays_hbm, blocks_hbm, pot_hbm, leak_hbm, drive_hbm,
    rates_ref, last_ref,
    hist_ref, weights, delays_ref, blocks_ref, pot_ref, leak_ref, drive_ref, hbuf, spans, sent, got, acc, xgot, zsend, zgot, src_area, tgt_area,
    in_sem, zsend_sem, zrecv_sem, ysend_sem, yrecv_sem, xsend_sem, xrecv_sem, hsend_sem, hrecv_sem,
):
    blk = lax.axis_index("blk")
    tgt = lax.axis_index("tgt")
    core = lax.rem(blk, 2)
    z = lax.rem(blk // 2, CHAIN)
    y = blk // (2 * CHAIN)
    x = tgt // 2
    z_hi = lax.rem(tgt, 2)

    def block_at(yy, zz, cc):
        return (yy * CHAIN + zz) * 2 + cc

    def peer_block(k, zz):
        dy, dc = k // 2, k % 2
        return block_at(lax.rem(y + dy, RING), zz, lax.rem(core + dc, 2))

    def x_peer(dx):
        return (blk, lax.rem(x + dx, RING) * 2 + z_hi)

    across = (blk, x * 2 + 1 - z_hi)
    right = (block_at(y, z + 1, core), tgt)
    left = (block_at(y, z - 1, core), tgt)

    pairs = [
        (hist_hbm, hist_ref), (blocks_hbm, blocks_ref), (delays_hbm, delays_ref), (weights_hbm, weights),
        (pot_hbm, pot_ref), (leak_hbm, leak_ref), (drive_hbm, drive_ref),
    ]
    loads = [pltpu.make_async_copy(a, b, in_sem.at[i]) for i, (a, b) in enumerate(pairs)]
    for load in loads:
        load.start()

    barrier = pltpu.get_barrier_semaphore()
    for k in range(1, PEERS):
        pl.semaphore_signal(barrier, 1, device_id=(peer_block(k, z), tgt), device_id_type=MESH)
    for dx in range(1, RING):
        pl.semaphore_signal(barrier, 1, device_id=x_peer(dx), device_id_type=MESH)
    pl.semaphore_signal(barrier, 1, device_id=across, device_id_type=MESH)

    @pl.when(z < CHAIN - 1)
    def _():
        pl.semaphore_signal(barrier, 1, device_id=right, device_id_type=MESH)

    @pl.when(z > 0)
    def _():
        pl.semaphore_signal(barrier, 1, device_id=left, device_id_type=MESH)

    width = STEPS * TRIALS
    row = lax.broadcasted_iota(jnp.int32, (width, width), 0)
    col = lax.broadcasted_iota(jnp.int32, (width, width), 1)
    inner = lax.rem(col, LANES)
    wanted = (inner // GROUP) * TRIALS + (col // LANES) * GROUP + lax.rem(inner, GROUP)
    regroup = jnp.where(row == wanted, 1.0, 0.0).astype(jnp.bfloat16)
    loads[0].wait()
    for q in range(SPANS):
        part = hist_ref[:, q * width : (q + 1) * width].astype(jnp.bfloat16)
        moved = jnp.dot(part, regroup, preferred_element_type=jnp.float32).astype(jnp.bfloat16)
        for c in range(PASSES):
            hbuf[c, 0, q] = moved[:, c * LANES : (c + 1) * LANES]

    pl.semaphore_wait(
        barrier, PEERS - 1 + RING - 1 + 1 + jnp.where(z < CHAIN - 1, 1, 0) + jnp.where(z > 0, 1, 0)
    )

    def source_of(t):
        both = jnp.minimum(z, CHAIN - 1 - z)
        dist = jnp.where(t <= 2 * both, (t + 1) // 2, t - both)
        from_left = jnp.where(t <= 2 * both, lax.rem(t, 2), jnp.where(z >= CHAIN // 2, 1, 0))
        return jnp.where(from_left == 1, z - dist, z + dist)

    def slot_at(zr, zs):
        both = jnp.minimum(zr, CHAIN - 1 - zr)
        dist = jnp.abs(zr - zs)
        return jnp.where(dist <= both, 2 * dist - jnp.where(zs < zr, 1, 0), dist + both)

    def chain_copy(c, t, zs, to_right):
        there = slot_at(z + 1 if to_right else z - 1, zs)
        return pltpu.make_async_remote_copy(
            src_ref=hbuf.at[c, t],
            dst_ref=hbuf.at[c, there],
            send_sem=zsend_sem.at[1 if to_right else 0, c, t],
            recv_sem=zrecv_sem.at[c, there],
            device_id=right if to_right else left,
            device_id_type=MESH,
        )

    def chain_arrival(c, t):
        return pltpu.make_async_remote_copy(
            src_ref=hbuf.at[c, t],
            dst_ref=hbuf.at[c, t],
            send_sem=zsend_sem.at[0, c, t],
            recv_sem=zrecv_sem.at[c, t],
            device_id=left,
            device_id_type=MESH,
        )

    def goes_right(zs):
        return jnp.logical_and(zs <= z, z < CHAIN - 1)

    def goes_left(zs):
        return jnp.logical_and(zs >= z, z > 0)

    def pass_on(c, t):
        zs = source_of(t)

        @pl.when(goes_right(zs))
        def _():
            chain_copy(c, t, zs, True).start()

        @pl.when(goes_left(zs))
        def _():
            chain_copy(c, t, zs, False).start()

    for c in range(PASSES):
        pass_on(c, 0)
    acc[...] = jnp.zeros_like(acc)

    sources = [block_at(y, zz, core) for zz in range(CHAIN)]
    targets = [peer_block(k, z) for k in range(PEERS)]

    def count(a, carry):
        edge, counts = carry[0] + blocks_ref[a], carry[1:]
        more = [n + jnp.where(edge <= b, 1, 0) for n, b in zip(counts, sources + targets)]
        return (edge, *more)

    loads[1].wait()
    counted = lax.fori_loop(0, AREAS, count, (jnp.int32(0),) * (1 + CHAIN + PEERS))[1:]
    for i in range(CHAIN):
        src_area[i] = jnp.minimum(counted[i], AREAS - 1)
    for i in range(PEERS):
        tgt_area[i] = jnp.minimum(counted[CHAIN + i], AREAS - 1)

    lane = lax.broadcasted_iota(jnp.int32, (SHARE, LANES), 1)

    def spread(c, t):
        @pl.when(t > 0)
        def _():
            chain_arrival(c, t).wait_recv()
            pass_on(c, t)

        area = src_area[source_of(t)]
        begins = [
            jnp.clip(HIST - delays_ref[tgt_area[k], area], 0, HIST - STEPS) for k in range(PEERS)
        ]
        for q in range(SPANS):
            spans[q] = hbuf[c, t, q].astype(SPAN_TYPE)
        for k in ORDER:
            span = begins[k] // STEPS
            skip = lax.rem(begins[k], STEPS) * GROUP
            turn = lax.rem(LANES - skip, LANES)
            first = pltpu.roll(spans[span], turn, 1)
            second = pltpu.roll(spans[jnp.minimum(span + 1, SPANS - 1)], turn, 1)
            window = jnp.where(lane < LANES - skip, first, second).astype(jnp.bfloat16)
            if k == 0:
                got[c, t, 0] = window
            else:
                sent[c, t, k - 1] = window
        for k in ORDER[:-1]:
            back = (RING - k // 2) % RING * 2 + k % 2
            pltpu.make_async_remote_copy(
                src_ref=sent.at[c, t, k - 1],
                dst_ref=got.at[c, t, back],
                send_sem=ysend_sem.at[c, t],
                recv_sem=yrecv_sem.at[c, t],
                device_id=(peer_block(k, z), tgt),
                device_id_type=MESH,
            ).start()

    def windows_copy(c, t):
        return pltpu.make_async_remote_copy(
            src_ref=sent.at[c, t],
            dst_ref=got.at[c, t, pl.ds(1, PEERS - 1)],
            send_sem=ysend_sem.at[c, t],
            recv_sem=yrecv_sem.at[c, t],
            device_id=(peer_block(1, z), tgt),
            device_id_type=MESH,
        )

    def product(c, t):
        windows_copy(c, t).wait_recv()
        zs = source_of(t)
        rows = got[c, t].reshape(PEERS * SHARE, LANES)
        columns = jnp.concatenate([weights[peer_block(k, zs)] for k in range(PEERS)], axis=0)
        sums = lax.dot_general(
            rows, columns, (((0,), (0,)), ((), ())), preferred_element_type=jnp.float32
        )
        for i in range(RING):
            acc[c, i] += sums[:, i * 2 * SHARE : (i + 1) * 2 * SHARE]

    def x_copy(c, dx):
        return pltpu.make_async_remote_copy(
            src_ref=acc.at[c, lax.rem(x + dx, RING)],
            dst_ref=xgot.at[c, RING - 1 - dx],
            send_sem=xsend_sem.at[c],
            recv_sem=xrecv_sem.at[c],
            device_id=x_peer(dx),
            device_id_type=MESH,
        )

    def x_all(c):
        return pltpu.make_async_remote_copy(
            src_ref=acc.at[c, pl.ds(0, RING - 1)],
            dst_ref=xgot.at[c],
            send_sem=xsend_sem.at[c],
            recv_sem=xrecv_sem.at[c],
            device_id=x_peer(1),
            device_id_type=MESH,
        )

    def z_copy(c):
        return pltpu.make_async_remote_copy(
            src_ref=zsend.at[c, 0],
            dst_ref=zgot.at[c],
            send_sem=hsend_sem.at[c],
            recv_sem=hrecv_sem.at[c],
            device_id=across,
            device_id_type=MESH,
        )

    def sum_x(c):
        x_all(c).wait_recv()
        total = acc[c, x] + xgot[c, 0] + xgot[c, 1] + xgot[c, 2]
        early, late = total[: LANES // 2], total[LANES // 2 :]
        share0 = jnp.where(lane < SHARE, early, pltpu.roll(late, SHARE, 1))
        share1 = jnp.where(lane < SHARE, pltpu.roll(early, SHARE, 1), late)
        zsend[c, z_hi] = share1
        zsend[c, 1 - z_hi] = share0
        z_copy(c).start()

    def integrate(c):
        z_copy(c).wait_recv()
        total = zsend[c, 1] + zgot[c]
        turned = pltpu.roll(total, SHARE, 1)
        mine = pl.ds(pl.multiple_of(c * GROUP, GROUP), GROUP)
        membrane = pot_ref[mine, :]
        leak, drive = leak_ref[...], drive_ref[...]
        for s in range(STEPS):
            half = total if s < STEPS // 2 else turned
            begin = s % (STEPS // 2) * GROUP
            synaptic = half[begin : begin + GROUP, :SHARE]
            membrane = membrane + leak * (drive - membrane + synaptic)
            rates_ref[s, mine, :] = jnp.maximum(membrane, 0.0) + jnp.log1p(jnp.exp(-jnp.abs(membrane)))
        last_ref[mine, :] = membrane

    for load in loads[2:]:
        load.wait()

    def slot(k, _):
        def one(c, _):
            t = k - OFFSET * c

            @pl.when(jnp.logical_and(t >= 0, t < CHAIN))
            def _():
                spread(c, t)

            return 0

        def two(c, _):
            t = k - OFFSET * c - LAG

            @pl.when(jnp.logical_and(t >= 0, t < CHAIN))
            def _():
                product(c, t)

            @pl.when(t == CHAIN - 1)
            def _():
                for dx in range(1, RING):
                    x_copy(c, dx).start()

            return 0

        def three(c, _):
            t = k - OFFSET * c - LAG

            @pl.when(t == CHAIN)
            def _():
                sum_x(c)

            @pl.when(t == CHAIN + 1)
            def _():
                integrate(c)

            return 0

        lax.fori_loop(0, PASSES, one, 0)
        lax.fori_loop(0, PASSES, three, 0)
        lax.fori_loop(0, PASSES, two, 0)
        return 0

    lax.fori_loop(0, OFFSET * (PASSES - 1) + CHAIN + LAG + 2, slot, 0)

    def drain(n, _):
        c, t = n // CHAIN, lax.rem(n, CHAIN)
        zs = source_of(t)

        @pl.when(goes_right(zs))
        def _():
            chain_copy(c, t, zs, True).wait_send()

        @pl.when(goes_left(zs))
        def _():
            chain_copy(c, t, zs, False).wait_send()

        windows_copy(c, t).wait_send()

        @pl.when(t == 0)
        def _():
            x_all(c).wait_send()
            z_copy(c).wait_send()

        return 0

    lax.fori_loop(0, PASSES * CHAIN, drain, 0)


def on_device(history, weights, delays, area_blocks, potential, leak, drive):
    vmem = pl.BlockSpec(memory_space=pltpu.VMEM)
    dma = pltpu.SemaphoreType.DMA
    bf16, f32 = jnp.bfloat16, jnp.float32
    return pl.pallas_call(
        kernel,
        out_shape=(
            pltpu.VMEM((STEPS, TRIALS, SHARE), f32),
            pltpu.VMEM((TRIALS, SHARE), f32),
        ),
        in_specs=[pl.BlockSpec(memory_space=pltpu.HBM)] * 7,
        out_specs=(vmem, vmem),
        scratch_shapes=[
            pltpu.VMEM(history.shape, f32),
            pltpu.VMEM(weights.shape, bf16),
            pltpu.SMEM(delays.shape, jnp.int32),
            pltpu.SMEM(area_blocks.shape, jnp.int32),
            pltpu.VMEM(potential.shape, f32),
            pltpu.VMEM((1, SHARE), f32),
            pltpu.VMEM((1, SHARE), f32),
            pltpu.VMEM((PASSES, CHAIN, SPANS, SHARE, LANES), bf16),
            pltpu.VMEM((SPANS, SHARE, LANES), SPAN_TYPE),
            pltpu.VMEM((PASSES, CHAIN, PEERS - 1, SHARE, LANES), bf16),
            pltpu.VMEM((PASSES, CHAIN, PEERS, SHARE, LANES), bf16),
            pltpu.VMEM((PASSES, RING, LANES, 2 * SHARE), f32),
            pltpu.VMEM((PASSES, RING - 1, LANES, 2 * SHARE), f32),
            pltpu.VMEM((PASSES, 2, LANES // 2, 2 * SHARE), f32),
            pltpu.VMEM((PASSES, LANES // 2, 2 * SHARE), f32),
            pltpu.SMEM((CHAIN,), jnp.int32),
            pltpu.SMEM((PEERS,), jnp.int32),
            dma((7,)),
            dma((2, PASSES, CHAIN)),
            dma((PASSES, CHAIN)),
            dma((PASSES, CHAIN)),
            dma((PASSES, CHAIN)),
            dma((PASSES,)),
            dma((PASSES,)),
            dma((PASSES,)),
            dma((PASSES,)),
        ],
        compiler_params=pltpu.CompilerParams(
            collective_id=0, has_side_effects=True, vmem_limit_bytes=56 * 2**20
        ),
        name="network_interval",
    )(history, weights, delays, area_blocks, potential, leak.reshape(1, -1), drive.reshape(1, -1))


def solution(mesh):
    in_specs = (
        P(("blk", "tgt"), None),
        P(None, "tgt", "blk"),
        P(),
        P(),
        P(None, ("blk", "tgt")),
        P(("blk", "tgt")),
        P(("blk", "tgt")),
    )
    out_specs = (P(None, None, ("blk", "tgt")), P(None, ("blk", "tgt")))
    return jax.shard_map(
        on_device, mesh=mesh, in_specs=in_specs, out_specs=out_specs, check_vma=False
    )
```

```python
import functools

import jax
import jax.numpy as jnp
from jax import lax
from jax.experimental import pallas as pl
from jax.experimental.pallas import tpu as pltpu
from jax.sharding import PartitionSpec as P

MESH = pl.DeviceIdType.MESH
STEPS = 16
TRIALS = 24
GROUP = 8
PASSES = TRIALS // GROUP
HIST = 64
SPANS = HIST // STEPS
SHARE = 64
CHAIN = 8
RING = 4
PEERS = 8
AREAS = 32
LANES = STEPS * GROUP
HEAD = 16
CODE_MAX = 32767.0
COARSE = 16.0
FINE = 32768.0
OFFSET = 0
SPAN_TYPE = jnp.bfloat16
ORDER = (4, 5, 2, 3, 6, 7, 1, 0)

LAG = 3


def kernel(
    hist_hbm, weights_hbm, delays_hbm, blocks_hbm, pot_hbm, leak_hbm, drive_hbm,
    rates_ref, last_ref,
    hist_ref, weights, delays_ref, blocks_ref, pot_ref, leak_ref, drive_ref, hbuf, spans, sent, got, acc, own, xsend, xgot, zsend, zgot, src_area, tgt_area,
    in_sem, zsend_sem, zrecv_sem, ysend_sem, yrecv_sem, xsend_sem, xrecv_sem, hsend_sem, hrecv_sem,
):
    blk = lax.axis_index("blk")
    tgt = lax.axis_index("tgt")
    core = lax.rem(blk, 2)
    z = lax.rem(blk // 2, CHAIN)
    y = blk // (2 * CHAIN)
    x = tgt // 2
    z_hi = lax.rem(tgt, 2)

    def block_at(yy, zz, cc):
        return (yy * CHAIN + zz) * 2 + cc

    def peer_block(k, zz):
        dy, dc = k // 2, k % 2
        return block_at(lax.rem(y + dy, RING), zz, lax.rem(core + dc, 2))

    def x_peer(dx):
        return (blk, lax.rem(x + dx, RING) * 2 + z_hi)

    across = (blk, x * 2 + 1 - z_hi)
    right = (block_at(y, z + 1, core), tgt)
    left = (block_at(y, z - 1, core), tgt)

    pairs = [
        (hist_hbm, hist_ref), (blocks_hbm, blocks_ref), (delays_hbm, delays_ref), (weights_hbm, weights),
        (pot_hbm, pot_ref), (leak_hbm, leak_ref), (drive_hbm, drive_ref),
    ]
    loads = [pltpu.make_async_copy(a, b, in_sem.at[i]) for i, (a, b) in enumerate(pairs)]
    for load in loads:
        load.start()

    barrier = pltpu.get_barrier_semaphore()
    for k in range(1, PEERS):
        pl.semaphore_signal(barrier, 1, device_id=(peer_block(k, z), tgt), device_id_type=MESH)
    for dx in range(1, RING):
        pl.semaphore_signal(barrier, 1, device_id=x_peer(dx), device_id_type=MESH)
    pl.semaphore_signal(barrier, 1, device_id=across, device_id_type=MESH)

    @pl.when(z < CHAIN - 1)
    def _():
        pl.semaphore_signal(barrier, 1, device_id=right, device_id_type=MESH)

    @pl.when(z > 0)
    def _():
        pl.semaphore_signal(barrier, 1, device_id=left, device_id_type=MESH)

    width = STEPS * TRIALS
    row = lax.broadcasted_iota(jnp.int32, (width, width), 0)
    col = lax.broadcasted_iota(jnp.int32, (width, width), 1)
    inner = lax.rem(col, LANES)
    wanted = (inner // GROUP) * TRIALS + (col // LANES) * GROUP + lax.rem(inner, GROUP)
    regroup = jnp.where(row == wanted, 1.0, 0.0).astype(jnp.bfloat16)
    loads[0].wait()
    for q in range(SPANS):
        part = hist_ref[:, q * width : (q + 1) * width].astype(jnp.bfloat16)
        moved = jnp.dot(part, regroup, preferred_element_type=jnp.float32).astype(jnp.bfloat16)
        for c in range(PASSES):
            hbuf[c, 0, q] = moved[:, c * LANES : (c + 1) * LANES]

    pl.semaphore_wait(
        barrier, PEERS - 1 + RING - 1 + 1 + jnp.where(z < CHAIN - 1, 1, 0) + jnp.where(z > 0, 1, 0)
    )

    def source_of(t):
        both = jnp.minimum(z, CHAIN - 1 - z)
        dist = jnp.where(t <= 2 * both, (t + 1) // 2, t - both)
        from_left = jnp.where(t <= 2 * both, lax.rem(t, 2), jnp.where(z >= CHAIN // 2, 1, 0))
        return jnp.where(from_left == 1, z - dist, z + dist)

    def slot_at(zr, zs):
        both = jnp.minimum(zr, CHAIN - 1 - zr)
        dist = jnp.abs(zr - zs)
        return jnp.where(dist <= both, 2 * dist - jnp.where(zs < zr, 1, 0), dist + both)

    def chain_copy(c, t, zs, to_right):
        there = slot_at(z + 1 if to_right else z - 1, zs)
        return pltpu.make_async_remote_copy(
            src_ref=hbuf.at[c, t],
            dst_ref=hbuf.at[c, there],
            send_sem=zsend_sem.at[1 if to_right else 0, c, t],
            recv_sem=zrecv_sem.at[c, there],
            device_id=right if to_right else left,
            device_id_type=MESH,
        )

    def chain_arrival(c, t):
        return pltpu.make_async_remote_copy(
            src_ref=hbuf.at[c, t],
            dst_ref=hbuf.at[c, t],
            send_sem=zsend_sem.at[0, c, t],
            recv_sem=zrecv_sem.at[c, t],
            device_id=left,
            device_id_type=MESH,
        )

    def goes_right(zs):
        return jnp.logical_and(zs <= z, z < CHAIN - 1)

    def goes_left(zs):
        return jnp.logical_and(zs >= z, z > 0)

    def pass_on(c, t):
        zs = source_of(t)

        @pl.when(goes_right(zs))
        def _():
            chain_copy(c, t, zs, True).start()

        @pl.when(goes_left(zs))
        def _():
            chain_copy(c, t, zs, False).start()

    for c in range(PASSES):
        pass_on(c, 0)
    acc[...] = jnp.zeros_like(acc)

    sources = [block_at(y, zz, core) for zz in range(CHAIN)]
    targets = [peer_block(k, z) for k in range(PEERS)]

    def count(a, carry):
        edge, counts = carry[0] + blocks_ref[a], carry[1:]
        more = [n + jnp.where(edge <= b, 1, 0) for n, b in zip(counts, sources + targets)]
        return (edge, *more)

    loads[1].wait()
    counted = lax.fori_loop(0, AREAS, count, (jnp.int32(0),) * (1 + CHAIN + PEERS))[1:]
    for i in range(CHAIN):
        src_area[i] = jnp.minimum(counted[i], AREAS - 1)
    for i in range(PEERS):
        tgt_area[i] = jnp.minimum(counted[CHAIN + i], AREAS - 1)

    lane = lax.broadcasted_iota(jnp.int32, (SHARE, LANES), 1)

    def spread(c, t):
        @pl.when(t > 0)
        def _():
            chain_arrival(c, t).wait_recv()
            pass_on(c, t)

        area = src_area[source_of(t)]
        begins = [
            jnp.clip(HIST - delays_ref[tgt_area[k], area], 0, HIST - STEPS) for k in range(PEERS)
        ]
        for q in range(SPANS):
            spans[q] = hbuf[c, t, q].astype(SPAN_TYPE)
        for k in ORDER:
            span = begins[k] // STEPS
            skip = lax.rem(begins[k], STEPS) * GROUP
            turn = lax.rem(LANES - skip, LANES)
            first = pltpu.roll(spans[span], turn, 1)
            second = pltpu.roll(spans[jnp.minimum(span + 1, SPANS - 1)], turn, 1)
            window = jnp.where(lane < LANES - skip, first, second).astype(jnp.bfloat16)
            if k == 0:
                got[c, t, 0] = window
            else:
                sent[c, t, k - 1] = window
        for k in ORDER[:-1]:
            back = (RING - k // 2) % RING * 2 + k % 2
            pltpu.make_async_remote_copy(
                src_ref=sent.at[c, t, k - 1],
                dst_ref=got.at[c, t, back],
                send_sem=ysend_sem.at[c, t],
                recv_sem=yrecv_sem.at[c, t],
                device_id=(peer_block(k, z), tgt),
                device_id_type=MESH,
            ).start()

    def windows_copy(c, t):
        return pltpu.make_async_remote_copy(
            src_ref=sent.at[c, t],
            dst_ref=got.at[c, t, pl.ds(1, PEERS - 1)],
            send_sem=ysend_sem.at[c, t],
            recv_sem=yrecv_sem.at[c, t],
            device_id=(peer_block(1, z), tgt),
            device_id_type=MESH,
        )

    def product(c, t):
        windows_copy(c, t).wait_recv()
        zs = source_of(t)
        rows = got[c, t].reshape(PEERS * SHARE, LANES)
        columns = jnp.concatenate([weights[peer_block(k, zs)] for k in range(PEERS)], axis=0)
        sums = lax.dot_general(
            rows, columns, (((0,), (0,)), ((), ())), preferred_element_type=jnp.float32
        )
        for i in range(RING):
            acc[c, i] += sums[:, i * 2 * SHARE : (i + 1) * 2 * SHARE]

    def encode(values):
        top, low = jnp.max(values, axis=0, keepdims=True), jnp.min(values, axis=0, keepdims=True)

        def split(v):
            coarse = jnp.clip(jnp.round(v * COARSE), -CODE_MAX, CODE_MAX)
            return coarse, jnp.clip(jnp.round((v * COARSE - coarse) * FINE), -CODE_MAX, CODE_MAX)

        middle = split(0.5 * (top + low))
        half = split(0.5 * (top - low) + 4.0 / (COARSE * FINE))
        row = lax.broadcasted_iota(jnp.int32, (HEAD, values.shape[1]), 0)
        head = jnp.zeros((HEAD, values.shape[1]), jnp.float32)
        for i, part in enumerate(middle + half):
            head = jnp.where(row == i, part, head)
        body = jnp.round((values - joined(*middle)) * (CODE_MAX / joined(*half)))
        codes = jnp.concatenate([jnp.clip(body, -CODE_MAX, CODE_MAX), head], axis=0)
        return codes.astype(jnp.int32).astype(jnp.int16)

    def joined(coarse, fine):
        return coarse * (1.0 / COARSE) + fine * (1.0 / (COARSE * FINE))

    def decode(codes):
        numbers = codes.astype(jnp.int32).astype(jnp.float32)
        rows = codes.shape[0] - HEAD
        head = [numbers[rows + i : rows + i + 1] for i in range(4)]
        return joined(*head[:2]) + numbers[:rows] * (joined(*head[2:]) * (1.0 / CODE_MAX))

    def x_copy(c, dx):
        return pltpu.make_async_remote_copy(
            src_ref=xsend.at[c, dx - 1],
            dst_ref=xgot.at[c, RING - 1 - dx],
            send_sem=xsend_sem.at[c],
            recv_sem=xrecv_sem.at[c],
            device_id=x_peer(dx),
            device_id_type=MESH,
        )

    def x_all(c):
        return pltpu.make_async_remote_copy(
            src_ref=xsend.at[c],
            dst_ref=xgot.at[c],
            send_sem=xsend_sem.at[c],
            recv_sem=xrecv_sem.at[c],
            device_id=x_peer(1),
            device_id_type=MESH,
        )

    def send_x(c):
        for dx in (2, 1, 3):
            xsend[c, dx - 1] = encode(acc[c, lax.rem(x + dx, RING)])
            x_copy(c, dx).start()

    def z_copy(c):
        return pltpu.make_async_remote_copy(
            src_ref=zsend.at[c],
            dst_ref=zgot.at[c],
            send_sem=hsend_sem.at[c],
            recv_sem=hrecv_sem.at[c],
            device_id=across,
            device_id_type=MESH,
        )

    def sum_x(c):
        x_all(c).wait_recv()
        total = acc[c, x] + decode(xgot[c, 0]) + decode(xgot[c, 1]) + decode(xgot[c, 2])
        early, late = total[: LANES // 2], total[LANES // 2 :]
        share0 = jnp.where(lane < SHARE, early, pltpu.roll(late, SHARE, 1))
        share1 = jnp.where(lane < SHARE, pltpu.roll(early, SHARE, 1), late)
        first = z_hi == 0
        zsend[c] = encode(jnp.where(first, share1, share0))
        z_copy(c).start()
        own[c] = jnp.where(first, share0, share1)

    def integrate(c):
        z_copy(c).wait_recv()
        total = own[c] + decode(zgot[c])
        turned = pltpu.roll(total, SHARE, 1)
        mine = pl.ds(pl.multiple_of(c * GROUP, GROUP), GROUP)
        membrane = pot_ref[mine, :]
        leak, drive = leak_ref[...], drive_ref[...]
        for s in range(STEPS):
            half = total if s < STEPS // 2 else turned
            begin = s % (STEPS // 2) * GROUP
            synaptic = half[begin : begin + GROUP, :SHARE]
            membrane = membrane + leak * (drive - membrane + synaptic)
            rates_ref[s, mine, :] = jnp.maximum(membrane, 0.0) + jnp.log1p(jnp.exp(-jnp.abs(membrane)))
        last_ref[mine, :] = membrane

    for load in loads[2:]:
        load.wait()

    def slot(k, _):
        def one(c, _):
            t = k - OFFSET * c

            @pl.when(jnp.logical_and(t >= 0, t < CHAIN))
            def _():
                spread(c, t)

            return 0

        def two(c, _):
            t = k - OFFSET * c - LAG

            @pl.when(jnp.logical_and(t >= 0, t < CHAIN))
            def _():
                product(c, t)

            @pl.when(t == CHAIN - 1)
            def _():
                send_x(c)

            return 0

        def three(c, _):
            t = k - OFFSET * c - LAG

            @pl.when(t == CHAIN)
            def _():
                sum_x(c)

            @pl.when(t == CHAIN + 1)
            def _():
                integrate(c)

            return 0

        lax.fori_loop(0, PASSES, one, 0)
        lax.fori_loop(0, PASSES, three, 0)
        lax.fori_loop(0, PASSES, two, 0)
        return 0

    lax.fori_loop(0, OFFSET * (PASSES - 1) + CHAIN + LAG + 2, slot, 0)

    def drain(n, _):
        c, t = n // CHAIN, lax.rem(n, CHAIN)
        zs = source_of(t)

        @pl.when(goes_right(zs))
        def _():
            chain_copy(c, t, zs, True).wait_send()

        @pl.when(goes_left(zs))
        def _():
            chain_copy(c, t, zs, False).wait_send()

        windows_copy(c, t).wait_send()

        @pl.when(t == 0)
        def _():
            x_all(c).wait_send()
            z_copy(c).wait_send()

        return 0

    lax.fori_loop(0, PASSES * CHAIN, drain, 0)


def on_device(history, weights, delays, area_blocks, potential, leak, drive):
    vmem = pl.BlockSpec(memory_space=pltpu.VMEM)
    dma = pltpu.SemaphoreType.DMA
    bf16, f32 = jnp.bfloat16, jnp.float32
    return pl.pallas_call(
        kernel,
        out_shape=(
            pltpu.VMEM((STEPS, TRIALS, SHARE), f32),
            pltpu.VMEM((TRIALS, SHARE), f32),
        ),
        in_specs=[pl.BlockSpec(memory_space=pltpu.HBM)] * 7,
        out_specs=(vmem, vmem),
        scratch_shapes=[
            pltpu.VMEM(history.shape, f32),
            pltpu.VMEM(weights.shape, bf16),
            pltpu.SMEM(delays.shape, jnp.int32),
            pltpu.SMEM(area_blocks.shape, jnp.int32),
            pltpu.VMEM(potential.shape, f32),
            pltpu.VMEM((1, SHARE), f32),
            pltpu.VMEM((1, SHARE), f32),
            pltpu.VMEM((PASSES, CHAIN, SPANS, SHARE, LANES), bf16),
            pltpu.VMEM((SPANS, SHARE, LANES), SPAN_TYPE),
            pltpu.VMEM((PASSES, CHAIN, PEERS - 1, SHARE, LANES), bf16),
            pltpu.VMEM((PASSES, CHAIN, PEERS, SHARE, LANES), bf16),
            pltpu.VMEM((PASSES, RING, LANES, 2 * SHARE), f32),
            pltpu.VMEM((PASSES, LANES // 2, 2 * SHARE), f32),
            pltpu.VMEM((PASSES, RING - 1, LANES + HEAD, 2 * SHARE), jnp.int16),
            pltpu.VMEM((PASSES, RING - 1, LANES + HEAD, 2 * SHARE), jnp.int16),
            pltpu.VMEM((PASSES, LANES // 2 + HEAD, 2 * SHARE), jnp.int16),
            pltpu.VMEM((PASSES, LANES // 2 + HEAD, 2 * SHARE), jnp.int16),
            pltpu.SMEM((CHAIN,), jnp.int32),
            pltpu.SMEM((PEERS,), jnp.int32),
            dma((7,)),
            dma((2, PASSES, CHAIN)),
            dma((PASSES, CHAIN)),
            dma((PASSES, CHAIN)),
            dma((PASSES, CHAIN)),
            dma((PASSES,)),
            dma((PASSES,)),
            dma((PASSES,)),
            dma((PASSES,)),
        ],
        compiler_params=pltpu.CompilerParams(
            collective_id=0, has_side_effects=True, vmem_limit_bytes=56 * 2**20
        ),
        name="network_interval",
    )(history, weights, delays, area_blocks, potential, leak.reshape(1, -1), drive.reshape(1, -1))


def solution(mesh):
    in_specs = (
        P(("blk", "tgt"), None),
        P(None, "tgt", "blk"),
        P(),
        P(),
        P(None, ("blk", "tgt")),
        P(("blk", "tgt")),
        P(("blk", "tgt")),
    )
    out_specs = (P(None, None, ("blk", "tgt")), P(None, ("blk", "tgt")))
    return jax.shard_map(
        on_device, mesh=mesh, in_specs=in_specs, out_specs=out_specs, check_vma=False
    )
```

```python
import functools

import jax
import jax.numpy as jnp
from jax import lax
from jax.experimental import pallas as pl
from jax.experimental.pallas import tpu as pltpu
from jax.sharding import PartitionSpec as P

MESH = pl.DeviceIdType.MESH
STEPS = 16
TRIALS = 24
GROUP = 8
PASSES = TRIALS // GROUP
HIST = 64
SPANS = HIST // STEPS
SHARE = 64
CHAIN = 8
RING = 4
PEERS = 8
AREAS = 32
LANES = STEPS * GROUP
HEAD = 16
CODE_MAX = 32767.0
COARSE = 16.0
FINE = 32768.0
OFFSET = 0
SPAN_TYPE = jnp.bfloat16
ORDER = (4, 5, 2, 3, 6, 7, 1, 0)

LAG = 3


def kernel(
    hist_hbm, weights_hbm, delays_hbm, blocks_hbm, pot_hbm, leak_hbm, drive_hbm,
    rates_ref, last_ref,
    hist_ref, weights, delays_ref, blocks_ref, pot_ref, leak_ref, drive_ref, hbuf, spans, sent, got, acc, own, xsend, xgot, zsend, zgot, src_area, tgt_area,
    in_sem, zsend_sem, zrecv_sem, ysend_sem, yrecv_sem, xsend_sem, xrecv_sem, hsend_sem, hrecv_sem,
):
    blk = lax.axis_index("blk")
    tgt = lax.axis_index("tgt")
    core = lax.rem(blk, 2)
    z = lax.rem(blk // 2, CHAIN)
    y = blk // (2 * CHAIN)
    x = tgt // 2
    z_hi = lax.rem(tgt, 2)

    def block_at(yy, zz, cc):
        return (yy * CHAIN + zz) * 2 + cc

    def peer_block(k, zz):
        dy, dc = k // 2, k % 2
        return block_at(lax.rem(y + dy, RING), zz, lax.rem(core + dc, 2))

    def x_peer(dx):
        return (blk, lax.rem(x + dx, RING) * 2 + z_hi)

    across = (blk, x * 2 + 1 - z_hi)
    right = (block_at(y, z + 1, core), tgt)
    left = (block_at(y, z - 1, core), tgt)

    pairs = [
        (hist_hbm, hist_ref), (blocks_hbm, blocks_ref), (delays_hbm, delays_ref), (pot_hbm, pot_ref),
        (leak_hbm, leak_ref), (drive_hbm, drive_ref), (weights_hbm, weights),
    ]
    loads = [pltpu.make_async_copy(a, b, in_sem.at[i]) for i, (a, b) in enumerate(pairs)]
    loads[0].start()
    barrier = pltpu.get_barrier_semaphore()
    pl.semaphore_signal(barrier, 1, device_id=across, device_id_type=MESH)

    @pl.when(z < CHAIN - 1)
    def _():
        pl.semaphore_signal(barrier, 1, device_id=right, device_id_type=MESH)

    @pl.when(z > 0)
    def _():
        pl.semaphore_signal(barrier, 1, device_id=left, device_id_type=MESH)

    for k in ORDER[:-1]:
        pl.semaphore_signal(barrier, 1, device_id=(peer_block(k, z), tgt), device_id_type=MESH)
    for dx in (2, 1, 3):
        pl.semaphore_signal(barrier, 1, device_id=x_peer(dx), device_id_type=MESH)
    for load in loads[1:-1]:
        load.start()

    width = STEPS * TRIALS
    row = lax.broadcasted_iota(jnp.int32, (width, width), 0)
    col = lax.broadcasted_iota(jnp.int32, (width, width), 1)
    inner = lax.rem(col, LANES)
    wanted = (inner // GROUP) * TRIALS + (col // LANES) * GROUP + lax.rem(inner, GROUP)
    regroup = jnp.where(row == wanted, 1.0, 0.0).astype(jnp.bfloat16)
    loads[0].wait()
    for q in range(SPANS):
        part = hist_ref[:, q * width : (q + 1) * width].astype(jnp.bfloat16)
        moved = jnp.dot(part, regroup, preferred_element_type=jnp.float32).astype(jnp.bfloat16)
        for c in range(PASSES):
            hbuf[c, 0, q] = moved[:, c * LANES : (c + 1) * LANES]

    pl.semaphore_wait(
        barrier, PEERS - 1 + RING - 1 + 1 + jnp.where(z < CHAIN - 1, 1, 0) + jnp.where(z > 0, 1, 0)
    )

    def source_of(t):
        both = jnp.minimum(z, CHAIN - 1 - z)
        dist = jnp.where(t <= 2 * both, (t + 1) // 2, t - both)
        from_left = jnp.where(t <= 2 * both, lax.rem(t, 2), jnp.where(z >= CHAIN // 2, 1, 0))
        return jnp.where(from_left == 1, z - dist, z + dist)

    def slot_at(zr, zs):
        both = jnp.minimum(zr, CHAIN - 1 - zr)
        dist = jnp.abs(zr - zs)
        return jnp.where(dist <= both, 2 * dist - jnp.where(zs < zr, 1, 0), dist + both)

    def chain_copy(c, t, zs, to_right):
        there = slot_at(z + 1 if to_right else z - 1, zs)
        return pltpu.make_async_remote_copy(
            src_ref=hbuf.at[c, t],
            dst_ref=hbuf.at[c, there],
            send_sem=zsend_sem.at[1 if to_right else 0, c, t],
            recv_sem=zrecv_sem.at[c, there],
            device_id=right if to_right else left,
            device_id_type=MESH,
        )

    def chain_arrival(c, t):
        return pltpu.make_async_remote_copy(
            src_ref=hbuf.at[c, t],
            dst_ref=hbuf.at[c, t],
            send_sem=zsend_sem.at[0, c, t],
            recv_sem=zrecv_sem.at[c, t],
            device_id=left,
            device_id_type=MESH,
        )

    def goes_right(zs):
        return jnp.logical_and(zs <= z, z < CHAIN - 1)

    def goes_left(zs):
        return jnp.logical_and(zs >= z, z > 0)

    def pass_on(c, t):
        zs = source_of(t)

        @pl.when(goes_right(zs))
        def _():
            chain_copy(c, t, zs, True).start()

        @pl.when(goes_left(zs))
        def _():
            chain_copy(c, t, zs, False).start()

    for c in range(PASSES):
        pass_on(c, 0)
    loads[-1].start()
    acc[...] = jnp.zeros_like(acc)

    sources = [block_at(y, zz, core) for zz in range(CHAIN)]
    targets = [peer_block(k, z) for k in range(PEERS)]

    def count(a, carry):
        edge, counts = carry[0] + blocks_ref[a], carry[1:]
        more = [n + jnp.where(edge <= b, 1, 0) for n, b in zip(counts, sources + targets)]
        return (edge, *more)

    loads[1].wait()
    counted = lax.fori_loop(0, AREAS, count, (jnp.int32(0),) * (1 + CHAIN + PEERS))[1:]
    for i in range(CHAIN):
        src_area[i] = jnp.minimum(counted[i], AREAS - 1)
    for i in range(PEERS):
        tgt_area[i] = jnp.minimum(counted[CHAIN + i], AREAS - 1)

    lane = lax.broadcasted_iota(jnp.int32, (SHARE, LANES), 1)

    def spread(c, t):
        @pl.when(t > 0)
        def _():
            chain_arrival(c, t).wait_recv()
            pass_on(c, t)

        area = src_area[source_of(t)]
        begins = [
            jnp.clip(HIST - delays_ref[tgt_area[k], area], 0, HIST - STEPS) for k in range(PEERS)
        ]
        for q in range(SPANS):
            spans[q] = hbuf[c, t, q].astype(SPAN_TYPE)
        for k in ORDER:
            span = begins[k] // STEPS
            skip = lax.rem(begins[k], STEPS) * GROUP
            turn = lax.rem(LANES - skip, LANES)
            first = pltpu.roll(spans[span], turn, 1)
            second = pltpu.roll(spans[jnp.minimum(span + 1, SPANS - 1)], turn, 1)
            window = jnp.where(lane < LANES - skip, first, second).astype(jnp.bfloat16)
            if k == 0:
                got[c, t, 0] = window
            else:
                sent[c, t, k - 1] = window
        for k in ORDER[:-1]:
            back = (RING - k // 2) % RING * 2 + k % 2
            pltpu.make_async_remote_copy(
                src_ref=sent.at[c, t, k - 1],
                dst_ref=got.at[c, t, back],
                send_sem=ysend_sem.at[c, t],
                recv_sem=yrecv_sem.at[c, t],
                device_id=(peer_block(k, z), tgt),
                device_id_type=MESH,
            ).start()

    def windows_copy(c, t):
        return pltpu.make_async_remote_copy(
            src_ref=sent.at[c, t],
            dst_ref=got.at[c, t, pl.ds(1, PEERS - 1)],
            send_sem=ysend_sem.at[c, t],
            recv_sem=yrecv_sem.at[c, t],
            device_id=(peer_block(1, z), tgt),
            device_id_type=MESH,
        )

    def product(c, t):
        windows_copy(c, t).wait_recv()
        zs = source_of(t)
        rows = got[c, t].reshape(PEERS * SHARE, LANES)
        columns = jnp.concatenate([weights[peer_block(k, zs)] for k in range(PEERS)], axis=0)
        sums = lax.dot_general(
            rows, columns, (((0,), (0,)), ((), ())), preferred_element_type=jnp.float32
        )
        for i in range(RING):
            acc[c, i] += sums[:, i * 2 * SHARE : (i + 1) * 2 * SHARE]

    def encode(values):
        top, low = jnp.max(values, axis=0, keepdims=True), jnp.min(values, axis=0, keepdims=True)

        def split(v):
            coarse = jnp.clip(jnp.round(v * COARSE), -CODE_MAX, CODE_MAX)
            return coarse, jnp.clip(jnp.round((v * COARSE - coarse) * FINE), -CODE_MAX, CODE_MAX)

        middle = split(0.5 * (top + low))
        half = split(0.5 * (top - low) + 4.0 / (COARSE * FINE))
        row = lax.broadcasted_iota(jnp.int32, (HEAD, values.shape[1]), 0)
        head = jnp.zeros((HEAD, values.shape[1]), jnp.float32)
        for i, part in enumerate(middle + half):
            head = jnp.where(row == i, part, head)
        body = jnp.round((values - joined(*middle)) * (CODE_MAX / joined(*half)))
        codes = jnp.concatenate([jnp.clip(body, -CODE_MAX, CODE_MAX), head], axis=0)
        return codes.astype(jnp.int32).astype(jnp.int16)

    def joined(coarse, fine):
        return coarse * (1.0 / COARSE) + fine * (1.0 / (COARSE * FINE))

    def decode(codes):
        numbers = codes.astype(jnp.int32).astype(jnp.float32)
        rows = codes.shape[0] - HEAD
        head = [numbers[rows + i : rows + i + 1] for i in range(4)]
        return joined(*head[:2]) + numbers[:rows] * (joined(*head[2:]) * (1.0 / CODE_MAX))

    def x_copy(c, dx):
        return pltpu.make_async_remote_copy(
            src_ref=xsend.at[c, dx - 1],
            dst_ref=xgot.at[c, RING - 1 - dx],
            send_sem=xsend_sem.at[c],
            recv_sem=xrecv_sem.at[c],
            device_id=x_peer(dx),
            device_id_type=MESH,
        )

    def x_all(c):
        return pltpu.make_async_remote_copy(
            src_ref=xsend.at[c],
            dst_ref=xgot.at[c],
            send_sem=xsend_sem.at[c],
            recv_sem=xrecv_sem.at[c],
            device_id=x_peer(1),
            device_id_type=MESH,
        )

    def send_x(c):
        for dx in (2, 1, 3):
            xsend[c, dx - 1] = encode(acc[c, lax.rem(x + dx, RING)])
            x_copy(c, dx).start()

    def z_copy(c):
        return pltpu.make_async_remote_copy(
            src_ref=zsend.at[c],
            dst_ref=zgot.at[c],
            send_sem=hsend_sem.at[c],
            recv_sem=hrecv_sem.at[c],
            device_id=across,
            device_id_type=MESH,
        )

    def sum_x(c):
        x_all(c).wait_recv()
        total = acc[c, x] + decode(xgot[c, 0]) + decode(xgot[c, 1]) + decode(xgot[c, 2])
        early, late = total[: LANES // 2], total[LANES // 2 :]
        share0 = jnp.where(lane < SHARE, early, pltpu.roll(late, SHARE, 1))
        share1 = jnp.where(lane < SHARE, pltpu.roll(early, SHARE, 1), late)
        first = z_hi == 0
        zsend[c] = encode(jnp.where(first, share1, share0))
        z_copy(c).start()
        own[c] = jnp.where(first, share0, share1)

    def integrate(c):
        z_copy(c).wait_recv()
        total = own[c] + decode(zgot[c])
        turned = pltpu.roll(total, SHARE, 1)
        mine = pl.ds(pl.multiple_of(c * GROUP, GROUP), GROUP)
        membrane = pot_ref[mine, :]
        leak, drive = leak_ref[...], drive_ref[...]
        for s in range(STEPS):
            half = total if s < STEPS // 2 else turned
            begin = s % (STEPS // 2) * GROUP
            synaptic = half[begin : begin + GROUP, :SHARE]
            membrane = membrane + leak * (drive - membrane + synaptic)
            rates_ref[s, mine, :] = jnp.maximum(membrane, 0.0) + jnp.log1p(jnp.exp(-jnp.abs(membrane)))
        last_ref[mine, :] = membrane

    loads[2].wait()

    def slot(k, _):
        def one(c, _):
            t = k - OFFSET * c

            @pl.when(jnp.logical_and(t >= 0, t < CHAIN))
            def _():
                spread(c, t)

            return 0

        def two(c, _):
            t = k - OFFSET * c - LAG

            @pl.when(jnp.logical_and(t == 0, c == 0))
            def _():
                for load in loads[3:]:
                    load.wait()

            @pl.when(jnp.logical_and(t >= 0, t < CHAIN))
            def _():
                product(c, t)

            @pl.when(t == CHAIN - 1)
            def _():
                send_x(c)

            return 0

        lax.fori_loop(0, PASSES, one, 0)
        lax.fori_loop(0, PASSES, two, 0)
        return 0

    lax.fori_loop(0, OFFSET * (PASSES - 1) + CHAIN + LAG, slot, 0)

    def drain(n, _):
        c, t = n // CHAIN, lax.rem(n, CHAIN)
        zs = source_of(t)

        @pl.when(goes_right(zs))
        def _():
            chain_copy(c, t, zs, True).wait_send()

        @pl.when(goes_left(zs))
        def _():
            chain_copy(c, t, zs, False).wait_send()

        windows_copy(c, t).wait_send()
        return 0

    lax.fori_loop(0, PASSES * CHAIN, drain, 0)
    for c in range(PASSES):
        sum_x(c)
    for c in range(PASSES):
        integrate(c)
    for c in range(PASSES):
        x_all(c).wait_send()
        z_copy(c).wait_send()


def on_device(history, weights, delays, area_blocks, potential, leak, drive):
    vmem = pl.BlockSpec(memory_space=pltpu.VMEM)
    dma = pltpu.SemaphoreType.DMA
    bf16, f32 = jnp.bfloat16, jnp.float32
    return pl.pallas_call(
        kernel,
        out_shape=(
            pltpu.VMEM((STEPS, TRIALS, SHARE), f32),
            pltpu.VMEM((TRIALS, SHARE), f32),
        ),
        in_specs=[pl.BlockSpec(memory_space=pltpu.HBM)] * 7,
        out_specs=(vmem, vmem),
        scratch_shapes=[
            pltpu.VMEM(history.shape, f32),
            pltpu.VMEM(weights.shape, bf16),
            pltpu.SMEM(delays.shape, jnp.int32),
            pltpu.SMEM(area_blocks.shape, jnp.int32),
            pltpu.VMEM(potential.shape, f32),
            pltpu.VMEM((1, SHARE), f32),
            pltpu.VMEM((1, SHARE), f32),
            pltpu.VMEM((PASSES, CHAIN, SPANS, SHARE, LANES), bf16),
            pltpu.VMEM((SPANS, SHARE, LANES), SPAN_TYPE),
            pltpu.VMEM((PASSES, CHAIN, PEERS - 1, SHARE, LANES), bf16),
            pltpu.VMEM((PASSES, CHAIN, PEERS, SHARE, LANES), bf16),
            pltpu.VMEM((PASSES, RING, LANES, 2 * SHARE), f32),
            pltpu.VMEM((PASSES, LANES // 2, 2 * SHARE), f32),
            pltpu.VMEM((PASSES, RING - 1, LANES + HEAD, 2 * SHARE), jnp.int16),
            pltpu.VMEM((PASSES, RING - 1, LANES + HEAD, 2 * SHARE), jnp.int16),
            pltpu.VMEM((PASSES, LANES // 2 + HEAD, 2 * SHARE), jnp.int16),
            pltpu.VMEM((PASSES, LANES // 2 + HEAD, 2 * SHARE), jnp.int16),
            pltpu.SMEM((CHAIN,), jnp.int32),
            pltpu.SMEM((PEERS,), jnp.int32),
            dma((7,)),
            dma((2, PASSES, CHAIN)),
            dma((PASSES, CHAIN)),
            dma((PASSES, CHAIN)),
            dma((PASSES, CHAIN)),
            dma((PASSES,)),
            dma((PASSES,)),
            dma((PASSES,)),
            dma((PASSES,)),
        ],
        compiler_params=pltpu.CompilerParams(
            collective_id=0, has_side_effects=True, vmem_limit_bytes=56 * 2**20
        ),
        name="network_interval",
    )(history, weights, delays, area_blocks, potential, leak.reshape(1, -1), drive.reshape(1, -1))


def solution(mesh):
    in_specs = (
        P(("blk", "tgt"), None),
        P(None, "tgt", "blk"),
        P(),
        P(),
        P(None, ("blk", "tgt")),
        P(("blk", "tgt")),
        P(("blk", "tgt")),
    )
    out_specs = (P(None, None, ("blk", "tgt")), P(None, ("blk", "tgt")))
    return jax.shard_map(
        on_device, mesh=mesh, in_specs=in_specs, out_specs=out_specs, check_vma=False
    )
```

```python
import functools

import jax
import jax.numpy as jnp
from jax import lax
from jax.experimental import pallas as pl
from jax.experimental.pallas import tpu as pltpu
from jax.sharding import PartitionSpec as P

MESH = pl.DeviceIdType.MESH
STEPS = 16
TRIALS = 24
GROUP = 8
PASSES = TRIALS // GROUP
HIST = 64
SPANS = HIST // STEPS
SHARE = 64
CHAIN = 8
RING = 4
PEERS = 8
AREAS = 32
LANES = STEPS * GROUP
HEAD = 16
CODE_MAX = 32767.0
COARSE = 16.0
FINE = 32768.0
OFFSET = 0
SPAN_TYPE = jnp.bfloat16
ORDER = (4, 5, 2, 3, 6, 7, 1, 0)

LAG = 3


def kernel(
    hist_hbm, weights_hbm, delays_hbm, blocks_hbm, pot_hbm, leak_hbm, drive_hbm,
    rates_ref, last_ref,
    hist_ref, weights, delays_ref, blocks_ref, pot_ref, leak_ref, drive_ref, hbuf, spans, sent, got, acc, own, xsend, xgot, zsend, zgot, src_area, tgt_area,
    in_sem, zsend_sem, zrecv_sem, ysend_sem, yrecv_sem, xsend_sem, xrecv_sem, hsend_sem, hrecv_sem,
):
    blk = lax.axis_index("blk")
    tgt = lax.axis_index("tgt")
    core = lax.rem(blk, 2)
    z = lax.rem(blk // 2, CHAIN)
    y = blk // (2 * CHAIN)
    x = tgt // 2
    z_hi = lax.rem(tgt, 2)

    def block_at(yy, zz, cc):
        return (yy * CHAIN + zz) * 2 + cc

    def peer_block(k, zz):
        dy, dc = k // 2, k % 2
        return block_at(lax.rem(y + dy, RING), zz, lax.rem(core + dc, 2))

    def x_peer(dx):
        return (blk, lax.rem(x + dx, RING) * 2 + z_hi)

    across = (blk, x * 2 + 1 - z_hi)
    right = (block_at(y, z + 1, core), tgt)
    left = (block_at(y, z - 1, core), tgt)

    pairs = [
        (hist_hbm, hist_ref), (blocks_hbm, blocks_ref), (delays_hbm, delays_ref), (pot_hbm, pot_ref),
        (leak_hbm, leak_ref), (drive_hbm, drive_ref), (weights_hbm, weights),
    ]
    loads = [pltpu.make_async_copy(a, b, in_sem.at[i]) for i, (a, b) in enumerate(pairs)]
    loads[0].start()
    loads[1].start()
    barrier = pltpu.get_barrier_semaphore()
    pl.semaphore_signal(barrier, 1, device_id=across, device_id_type=MESH)

    @pl.when(z < CHAIN - 1)
    def _():
        pl.semaphore_signal(barrier, 1, device_id=right, device_id_type=MESH)

    @pl.when(z > 0)
    def _():
        pl.semaphore_signal(barrier, 1, device_id=left, device_id_type=MESH)

    for k in ORDER[:-1]:
        pl.semaphore_signal(barrier, 1, device_id=(peer_block(k, z), tgt), device_id_type=MESH)
    for dx in (2, 1, 3):
        pl.semaphore_signal(barrier, 1, device_id=x_peer(dx), device_id_type=MESH)
    for load in loads[2:-1]:
        load.start()

    width = STEPS * TRIALS
    row = lax.broadcasted_iota(jnp.int32, (width, width), 0)
    col = lax.broadcasted_iota(jnp.int32, (width, width), 1)
    inner = lax.rem(col, LANES)
    wanted = (inner // GROUP) * TRIALS + (col // LANES) * GROUP + lax.rem(inner, GROUP)
    regroup = jnp.where(row == wanted, 1.0, 0.0).astype(jnp.bfloat16)
    sources = [block_at(y, zz, core) for zz in range(CHAIN)]
    targets = [peer_block(k, z) for k in range(PEERS)]

    def count(a, carry):
        edge, counts = carry[0] + blocks_ref[a], carry[1:]
        more = [n + jnp.where(edge <= b, 1, 0) for n, b in zip(counts, sources + targets)]
        return (edge, *more)

    loads[1].wait()
    counted = lax.fori_loop(0, AREAS, count, (jnp.int32(0),) * (1 + CHAIN + PEERS))[1:]
    for i in range(CHAIN):
        src_area[i] = jnp.minimum(counted[i], AREAS - 1)
    for i in range(PEERS):
        tgt_area[i] = jnp.minimum(counted[CHAIN + i], AREAS - 1)
    acc[...] = jnp.zeros_like(acc)

    loads[0].wait()
    for q in range(SPANS):
        part = hist_ref[:, q * width : (q + 1) * width].astype(jnp.bfloat16)
        moved = jnp.dot(part, regroup, preferred_element_type=jnp.float32).astype(jnp.bfloat16)
        for c in range(PASSES):
            hbuf[c, 0, q] = moved[:, c * LANES : (c + 1) * LANES]

    pl.semaphore_wait(
        barrier, PEERS - 1 + RING - 1 + 1 + jnp.where(z < CHAIN - 1, 1, 0) + jnp.where(z > 0, 1, 0)
    )

    def source_of(t):
        both = jnp.minimum(z, CHAIN - 1 - z)
        dist = jnp.where(t <= 2 * both, (t + 1) // 2, t - both)
        from_left = jnp.where(t <= 2 * both, lax.rem(t, 2), jnp.where(z >= CHAIN // 2, 1, 0))
        return jnp.where(from_left == 1, z - dist, z + dist)

    def slot_at(zr, zs):
        both = jnp.minimum(zr, CHAIN - 1 - zr)
        dist = jnp.abs(zr - zs)
        return jnp.where(dist <= both, 2 * dist - jnp.where(zs < zr, 1, 0), dist + both)

    def chain_copy(c, t, zs, to_right):
        there = slot_at(z + 1 if to_right else z - 1, zs)
        return pltpu.make_async_remote_copy(
            src_ref=hbuf.at[c, t],
            dst_ref=hbuf.at[c, there],
            send_sem=zsend_sem.at[1 if to_right else 0, c, t],
            recv_sem=zrecv_sem.at[c, there],
            device_id=right if to_right else left,
            device_id_type=MESH,
        )

    def chain_arrival(c, t):
        return pltpu.make_async_remote_copy(
            src_ref=hbuf.at[c, t],
            dst_ref=hbuf.at[c, t],
            send_sem=zsend_sem.at[0, c, t],
            recv_sem=zrecv_sem.at[c, t],
            device_id=left,
            device_id_type=MESH,
        )

    def goes_right(zs):
        return jnp.logical_and(zs <= z, z < CHAIN - 1)

    def goes_left(zs):
        return jnp.logical_and(zs >= z, z > 0)

    def pass_on(c, t):
        zs = source_of(t)

        @pl.when(goes_right(zs))
        def _():
            chain_copy(c, t, zs, True).start()

        @pl.when(goes_left(zs))
        def _():
            chain_copy(c, t, zs, False).start()

    for c in range(PASSES):
        pass_on(c, 0)
    loads[-1].start()

    lane = lax.broadcasted_iota(jnp.int32, (SHARE, LANES), 1)

    def spread(c, t):
        @pl.when(t > 0)
        def _():
            chain_arrival(c, t).wait_recv()
            pass_on(c, t)

        area = src_area[source_of(t)]
        begins = [
            jnp.clip(HIST - delays_ref[tgt_area[k], area], 0, HIST - STEPS) for k in range(PEERS)
        ]
        for q in range(SPANS):
            spans[q] = hbuf[c, t, q].astype(SPAN_TYPE)
        for k in ORDER:
            span = begins[k] // STEPS
            skip = lax.rem(begins[k], STEPS) * GROUP
            turn = lax.rem(LANES - skip, LANES)
            first = pltpu.roll(spans[span], turn, 1)
            second = pltpu.roll(spans[jnp.minimum(span + 1, SPANS - 1)], turn, 1)
            window = jnp.where(lane < LANES - skip, first, second).astype(jnp.bfloat16)
            if k == 0:
                got[c, t, 0] = window
            else:
                sent[c, t, k - 1] = window
        for k in ORDER[:-1]:
            back = (RING - k // 2) % RING * 2 + k % 2
            pltpu.make_async_remote_copy(
                src_ref=sent.at[c, t, k - 1],
                dst_ref=got.at[c, t, back],
                send_sem=ysend_sem.at[c, t],
                recv_sem=yrecv_sem.at[c, t],
                device_id=(peer_block(k, z), tgt),
                device_id_type=MESH,
            ).start()

    def windows_copy(c, t):
        return pltpu.make_async_remote_copy(
            src_ref=sent.at[c, t],
            dst_ref=got.at[c, t, pl.ds(1, PEERS - 1)],
            send_sem=ysend_sem.at[c, t],
            recv_sem=yrecv_sem.at[c, t],
            device_id=(peer_block(1, z), tgt),
            device_id_type=MESH,
        )

    def product(c, t):
        windows_copy(c, t).wait_recv()
        zs = source_of(t)
        rows = got[c, t].reshape(PEERS * SHARE, LANES)
        columns = jnp.concatenate([weights[peer_block(k, zs)] for k in range(PEERS)], axis=0)
        sums = lax.dot_general(
            rows, columns, (((0,), (0,)), ((), ())), preferred_element_type=jnp.float32
        )
        for i in range(RING):
            acc[c, i] += sums[:, i * 2 * SHARE : (i + 1) * 2 * SHARE]

    def encode(values):
        top, low = jnp.max(values, axis=0, keepdims=True), jnp.min(values, axis=0, keepdims=True)

        def split(v):
            coarse = jnp.clip(jnp.round(v * COARSE), -CODE_MAX, CODE_MAX)
            return coarse, jnp.clip(jnp.round((v * COARSE - coarse) * FINE), -CODE_MAX, CODE_MAX)

        middle = split(0.5 * (top + low))
        half = split(0.5 * (top - low) + 4.0 / (COARSE * FINE))
        row = lax.broadcasted_iota(jnp.int32, (HEAD, values.shape[1]), 0)
        head = jnp.zeros((HEAD, values.shape[1]), jnp.float32)
        for i, part in enumerate(middle + half):
            head = jnp.where(row == i, part, head)
        body = jnp.round((values - joined(*middle)) * (CODE_MAX / joined(*half)))
        codes = jnp.concatenate([jnp.clip(body, -CODE_MAX, CODE_MAX), head], axis=0)
        return codes.astype(jnp.int32).astype(jnp.int16)

    def joined(coarse, fine):
        return coarse * (1.0 / COARSE) + fine * (1.0 / (COARSE * FINE))

    def decode(codes):
        numbers = codes.astype(jnp.int32).astype(jnp.float32)
        rows = codes.shape[0] - HEAD
        head = [numbers[rows + i : rows + i + 1] for i in range(4)]
        return joined(*head[:2]) + numbers[:rows] * (joined(*head[2:]) * (1.0 / CODE_MAX))

    def x_copy(c, dx):
        return pltpu.make_async_remote_copy(
            src_ref=xsend.at[c, dx - 1],
            dst_ref=xgot.at[c, RING - 1 - dx],
            send_sem=xsend_sem.at[c],
            recv_sem=xrecv_sem.at[c],
            device_id=x_peer(dx),
            device_id_type=MESH,
        )

    def x_all(c):
        return pltpu.make_async_remote_copy(
            src_ref=xsend.at[c],
            dst_ref=xgot.at[c],
            send_sem=xsend_sem.at[c],
            recv_sem=xrecv_sem.at[c],
            device_id=x_peer(1),
            device_id_type=MESH,
        )

    def send_x(c):
        for dx in (2, 1, 3):
            xsend[c, dx - 1] = encode(acc[c, lax.rem(x + dx, RING)])
            x_copy(c, dx).start()

    def z_copy(c):
        return pltpu.make_async_remote_copy(
            src_ref=zsend.at[c],
            dst_ref=zgot.at[c],
            send_sem=hsend_sem.at[c],
            recv_sem=hrecv_sem.at[c],
            device_id=across,
            device_id_type=MESH,
        )

    def sum_x(c):
        x_all(c).wait_recv()
        total = acc[c, x] + decode(xgot[c, 0]) + decode(xgot[c, 1]) + decode(xgot[c, 2])
        early, late = total[: LANES // 2], total[LANES // 2 :]
        share0 = jnp.where(lane < SHARE, early, pltpu.roll(late, SHARE, 1))
        share1 = jnp.where(lane < SHARE, pltpu.roll(early, SHARE, 1), late)
        first = z_hi == 0
        zsend[c] = encode(jnp.where(first, share1, share0))
        z_copy(c).start()
        own[c] = jnp.where(first, share0, share1)

    def integrate(c):
        z_copy(c).wait_recv()
        total = own[c] + decode(zgot[c])
        turned = pltpu.roll(total, SHARE, 1)
        mine = pl.ds(pl.multiple_of(c * GROUP, GROUP), GROUP)
        membrane = pot_ref[mine, :]
        leak, drive = leak_ref[...], drive_ref[...]
        for s in range(STEPS):
            half = total if s < STEPS // 2 else turned
            begin = s % (STEPS // 2) * GROUP
            synaptic = half[begin : begin + GROUP, :SHARE]
            membrane = membrane + leak * (drive - membrane + synaptic)
            rates_ref[s, mine, :] = jnp.maximum(membrane, 0.0) + jnp.log1p(jnp.exp(-jnp.abs(membrane)))
        last_ref[mine, :] = membrane

    loads[2].wait()

    def slot(k, _):
        def one(c, _):
            t = k - OFFSET * c

            @pl.when(jnp.logical_and(t >= 0, t < CHAIN))
            def _():
                spread(c, t)

            return 0

        def two(c, _):
            t = k - OFFSET * c - LAG

            @pl.when(jnp.logical_and(t == 0, c == 0))
            def _():
                for load in loads[3:]:
                    load.wait()

            @pl.when(jnp.logical_and(t >= 0, t < CHAIN))
            def _():
                product(c, t)

            @pl.when(t == CHAIN - 1)
            def _():
                send_x(c)

            return 0

        lax.fori_loop(0, PASSES, one, 0)
        lax.fori_loop(0, PASSES, two, 0)
        return 0

    lax.fori_loop(0, OFFSET * (PASSES - 1) + CHAIN + LAG, slot, 0)

    def drain(n, _):
        c, t = n // CHAIN, lax.rem(n, CHAIN)
        zs = source_of(t)

        @pl.when(goes_right(zs))
        def _():
            chain_copy(c, t, zs, True).wait_send()

        @pl.when(goes_left(zs))
        def _():
            chain_copy(c, t, zs, False).wait_send()

        windows_copy(c, t).wait_send()
        return 0

    for c in range(PASSES):
        sum_x(c)
    lax.fori_loop(0, PASSES * CHAIN, drain, 0)
    for c in range(PASSES):
        integrate(c)
    for c in range(PASSES):
        x_all(c).wait_send()
        z_copy(c).wait_send()


def on_device(history, weights, delays, area_blocks, potential, leak, drive):
    vmem = pl.BlockSpec(memory_space=pltpu.VMEM)
    dma = pltpu.SemaphoreType.DMA
    bf16, f32 = jnp.bfloat16, jnp.float32
    return pl.pallas_call(
        kernel,
        out_shape=(
            pltpu.VMEM((STEPS, TRIALS, SHARE), f32),
            pltpu.VMEM((TRIALS, SHARE), f32),
        ),
        in_specs=[pl.BlockSpec(memory_space=pltpu.HBM)] * 7,
        out_specs=(vmem, vmem),
        scratch_shapes=[
            pltpu.VMEM(history.shape, f32),
            pltpu.VMEM(weights.shape, bf16),
            pltpu.SMEM(delays.shape, jnp.int32),
            pltpu.SMEM(area_blocks.shape, jnp.int32),
            pltpu.VMEM(potential.shape, f32),
            pltpu.VMEM((1, SHARE), f32),
            pltpu.VMEM((1, SHARE), f32),
            pltpu.VMEM((PASSES, CHAIN, SPANS, SHARE, LANES), bf16),
            pltpu.VMEM((SPANS, SHARE, LANES), SPAN_TYPE),
            pltpu.VMEM((PASSES, CHAIN, PEERS - 1, SHARE, LANES), bf16),
            pltpu.VMEM((PASSES, CHAIN, PEERS, SHARE, LANES), bf16),
            pltpu.VMEM((PASSES, RING, LANES, 2 * SHARE), f32),
            pltpu.VMEM((PASSES, LANES // 2, 2 * SHARE), f32),
            pltpu.VMEM((PASSES, RING - 1, LANES + HEAD, 2 * SHARE), jnp.int16),
            pltpu.VMEM((PASSES, RING - 1, LANES + HEAD, 2 * SHARE), jnp.int16),
            pltpu.VMEM((PASSES, LANES // 2 + HEAD, 2 * SHARE), jnp.int16),
            pltpu.VMEM((PASSES, LANES // 2 + HEAD, 2 * SHARE), jnp.int16),
            pltpu.SMEM((CHAIN,), jnp.int32),
            pltpu.SMEM((PEERS,), jnp.int32),
            dma((7,)),
            dma((2, PASSES, CHAIN)),
            dma((PASSES, CHAIN)),
            dma((PASSES, CHAIN)),
            dma((PASSES, CHAIN)),
            dma((PASSES,)),
            dma((PASSES,)),
            dma((PASSES,)),
            dma((PASSES,)),
        ],
        compiler_params=pltpu.CompilerParams(
            collective_id=0, has_side_effects=True, vmem_limit_bytes=56 * 2**20
        ),
        name="network_interval",
    )(history, weights, delays, area_blocks, potential, leak.reshape(1, -1), drive.reshape(1, -1))


def solution(mesh):
    in_specs = (
        P(("blk", "tgt"), None),
        P(None, "tgt", "blk"),
        P(),
        P(),
        P(None, ("blk", "tgt")),
        P(("blk", "tgt")),
        P(("blk", "tgt")),
    )
    out_specs = (P(None, None, ("blk", "tgt")), P(None, ("blk", "tgt")))
    return jax.shard_map(
        on_device, mesh=mesh, in_specs=in_specs, out_specs=out_specs, check_vma=False
    )
```

```python
import functools

import jax
import jax.numpy as jnp
from jax import lax
from jax.experimental import pallas as pl
from jax.experimental.pallas import tpu as pltpu
from jax.sharding import PartitionSpec as P

MESH = pl.DeviceIdType.MESH
STEPS = 16
TRIALS = 24
GROUP = 8
PASSES = TRIALS // GROUP
HIST = 64
SPANS = HIST // STEPS
SHARE = 64
CHAIN = 8
RING = 4
PEERS = 8
AREAS = 32
LANES = STEPS * GROUP
HEAD = 16
CODE_MAX = 32767.0
COARSE = 16.0
FINE = 32768.0
OFFSET = 0
SPAN_TYPE = jnp.bfloat16
ORDER = (4, 5, 2, 3, 6, 7, 1, 0)

LAG = 3


def kernel(
    hist_hbm, weights_hbm, delays_hbm, blocks_hbm, pot_hbm, leak_hbm, drive_hbm,
    rates_ref, last_ref,
    hist_ref, weights, delays_ref, blocks_ref, pot_ref, leak_ref, drive_ref, hbuf, spans, sent, got, acc, own, xsend, xgot, zsend, zgot, src_area, tgt_area,
    in_sem, zsend_sem, zrecv_sem, ysend_sem, yrecv_sem, xsend_sem, xrecv_sem, hsend_sem, hrecv_sem,
):
    blk = lax.axis_index("blk")
    tgt = lax.axis_index("tgt")
    core = lax.rem(blk, 2)
    z = lax.rem(blk // 2, CHAIN)
    y = blk // (2 * CHAIN)
    x = tgt // 2
    z_hi = lax.rem(tgt, 2)

    def block_at(yy, zz, cc):
        return (yy * CHAIN + zz) * 2 + cc

    def peer_block(k, zz):
        dy, dc = k // 2, k % 2
        return block_at(lax.rem(y + dy, RING), zz, lax.rem(core + dc, 2))

    def x_peer(dx):
        return (blk, lax.rem(x + dx, RING) * 2 + z_hi)

    across = (blk, x * 2 + 1 - z_hi)
    right = (block_at(y, z + 1, core), tgt)
    left = (block_at(y, z - 1, core), tgt)

    pairs = [
        (hist_hbm, hist_ref), (blocks_hbm, blocks_ref), (delays_hbm, delays_ref), (pot_hbm, pot_ref),
        (leak_hbm, leak_ref), (drive_hbm, drive_ref), (weights_hbm, weights),
    ]
    loads = [pltpu.make_async_copy(a, b, in_sem.at[i]) for i, (a, b) in enumerate(pairs)]
    loads[0].start()
    loads[1].start()
    barrier = pltpu.get_barrier_semaphore()
    pl.semaphore_signal(barrier, 1, device_id=across, device_id_type=MESH)

    @pl.when(z < CHAIN - 1)
    def _():
        pl.semaphore_signal(barrier, 1, device_id=right, device_id_type=MESH)

    @pl.when(z > 0)
    def _():
        pl.semaphore_signal(barrier, 1, device_id=left, device_id_type=MESH)

    for k in ORDER[:-1]:
        pl.semaphore_signal(barrier, 1, device_id=(peer_block(k, z), tgt), device_id_type=MESH)
    for dx in (2, 1, 3):
        pl.semaphore_signal(barrier, 1, device_id=x_peer(dx), device_id_type=MESH)
    for load in loads[2:-1]:
        load.start()

    width = STEPS * TRIALS
    row = lax.broadcasted_iota(jnp.int32, (width, width), 0)
    col = lax.broadcasted_iota(jnp.int32, (1, width), 1)
    inner = lax.rem(col, LANES)
    wanted = (inner // GROUP) * TRIALS + (col // LANES) * GROUP + lax.rem(inner, GROUP)
    regroup = jnp.where(row == wanted, 1.0, 0.0).astype(jnp.bfloat16)
    sources = [block_at(y, zz, core) for zz in range(CHAIN)]
    targets = [peer_block(k, z) for k in range(PEERS)]

    def count(a, carry):
        edge, counts = carry[0] + blocks_ref[a], carry[1:]
        more = [n + jnp.where(edge <= b, 1, 0) for n, b in zip(counts, sources + targets)]
        return (edge, *more)

    loads[1].wait()
    counted = lax.fori_loop(0, AREAS, count, (jnp.int32(0),) * (1 + CHAIN + PEERS))[1:]
    for i in range(CHAIN):
        src_area[i] = jnp.minimum(counted[i], AREAS - 1)
    for i in range(PEERS):
        tgt_area[i] = jnp.minimum(counted[CHAIN + i], AREAS - 1)
    acc[...] = jnp.zeros_like(acc)

    loads[0].wait()
    for q in range(SPANS):
        part = hist_ref[:, q * width : (q + 1) * width].astype(jnp.bfloat16)
        moved = jnp.dot(part, regroup, preferred_element_type=jnp.float32).astype(jnp.bfloat16)
        for c in range(PASSES):
            hbuf[c, 0, q] = moved[:, c * LANES : (c + 1) * LANES]

    pl.semaphore_wait(
        barrier, PEERS - 1 + RING - 1 + 1 + jnp.where(z < CHAIN - 1, 1, 0) + jnp.where(z > 0, 1, 0)
    )

    def source_of(t):
        both = jnp.minimum(z, CHAIN - 1 - z)
        dist = jnp.where(t <= 2 * both, (t + 1) // 2, t - both)
        from_left = jnp.where(t <= 2 * both, lax.rem(t, 2), jnp.where(z >= CHAIN // 2, 1, 0))
        return jnp.where(from_left == 1, z - dist, z + dist)

    def slot_at(zr, zs):
        both = jnp.minimum(zr, CHAIN - 1 - zr)
        dist = jnp.abs(zr - zs)
        return jnp.where(dist <= both, 2 * dist - jnp.where(zs < zr, 1, 0), dist + both)

    def chain_copy(c, t, zs, to_right):
        there = slot_at(z + 1 if to_right else z - 1, zs)
        return pltpu.make_async_remote_copy(
            src_ref=hbuf.at[c, t],
            dst_ref=hbuf.at[c, there],
            send_sem=zsend_sem.at[1 if to_right else 0, c, t],
            recv_sem=zrecv_sem.at[c, there],
            device_id=right if to_right else left,
            device_id_type=MESH,
        )

    def chain_arrival(c, t):
        return pltpu.make_async_remote_copy(
            src_ref=hbuf.at[c, t],
            dst_ref=hbuf.at[c, t],
            send_sem=zsend_sem.at[0, c, t],
            recv_sem=zrecv_sem.at[c, t],
            device_id=left,
            device_id_type=MESH,
        )

    def goes_right(zs):
        return jnp.logical_and(zs <= z, z < CHAIN - 1)

    def goes_left(zs):
        return jnp.logical_and(zs >= z, z > 0)

    def pass_on(c, t):
        zs = source_of(t)

        @pl.when(goes_right(zs))
        def _():
            chain_copy(c, t, zs, True).start()

        @pl.when(goes_left(zs))
        def _():
            chain_copy(c, t, zs, False).start()

    for c in range(PASSES):
        pass_on(c, 0)
    loads[-1].start()

    lane = lax.broadcasted_iota(jnp.int32, (SHARE, LANES), 1)

    def spread(c, t):
        @pl.when(t > 0)
        def _():
            chain_arrival(c, t).wait_recv()
            pass_on(c, t)

        area = src_area[source_of(t)]
        begins = [
            jnp.clip(HIST - delays_ref[tgt_area[k], area], 0, HIST - STEPS) for k in range(PEERS)
        ]
        for q in range(SPANS):
            spans[q] = hbuf[c, t, q].astype(SPAN_TYPE)
        for k in ORDER:
            span = begins[k] // STEPS
            skip = lax.rem(begins[k], STEPS) * GROUP
            turn = lax.rem(LANES - skip, LANES)
            first = pltpu.roll(spans[span], turn, 1)
            second = pltpu.roll(spans[jnp.minimum(span + 1, SPANS - 1)], turn, 1)
            window = jnp.where(lane < LANES - skip, first, second).astype(jnp.bfloat16)
            if k == 0:
                got[c, t, 0] = window
            else:
                sent[c, t, k - 1] = window
        for k in ORDER[:-1]:
            back = (RING - k // 2) % RING * 2 + k % 2
            pltpu.make_async_remote_copy(
                src_ref=sent.at[c, t, k - 1],
                dst_ref=got.at[c, t, back],
                send_sem=ysend_sem.at[c, t],
                recv_sem=yrecv_sem.at[c, t],
                device_id=(peer_block(k, z), tgt),
                device_id_type=MESH,
            ).start()

    def windows_copy(c, t):
        return pltpu.make_async_remote_copy(
            src_ref=sent.at[c, t],
            dst_ref=got.at[c, t, pl.ds(1, PEERS - 1)],
            send_sem=ysend_sem.at[c, t],
            recv_sem=yrecv_sem.at[c, t],
            device_id=(peer_block(1, z), tgt),
            device_id_type=MESH,
        )

    def product(c, t):
        windows_copy(c, t).wait_recv()
        zs = source_of(t)
        rows = got[c, t].reshape(PEERS * SHARE, LANES)
        columns = jnp.concatenate([weights[peer_block(k, zs)] for k in range(PEERS)], axis=0)
        sums = lax.dot_general(
            rows, columns, (((0,), (0,)), ((), ())), preferred_element_type=jnp.float32
        )
        for i in range(RING):
            acc[c, i] += sums[:, i * 2 * SHARE : (i + 1) * 2 * SHARE]

    def encode(values):
        top, low = jnp.max(values, axis=0, keepdims=True), jnp.min(values, axis=0, keepdims=True)

        def split(v):
            coarse = jnp.clip(jnp.round(v * COARSE), -CODE_MAX, CODE_MAX)
            return coarse, jnp.clip(jnp.round((v * COARSE - coarse) * FINE), -CODE_MAX, CODE_MAX)

        middle = split(0.5 * (top + low))
        half = split(0.5 * (top - low) + 4.0 / (COARSE * FINE))
        row = lax.broadcasted_iota(jnp.int32, (HEAD, values.shape[1]), 0)
        head = jnp.zeros((HEAD, values.shape[1]), jnp.float32)
        for i, part in enumerate(middle + half):
            head = jnp.where(row == i, part, head)
        body = jnp.round((values - joined(*middle)) * (CODE_MAX / joined(*half)))
        codes = jnp.concatenate([jnp.clip(body, -CODE_MAX, CODE_MAX), head], axis=0)
        return codes.astype(jnp.int32).astype(jnp.int16)

    def joined(coarse, fine):
        return coarse * (1.0 / COARSE) + fine * (1.0 / (COARSE * FINE))

    def decode(codes):
        numbers = codes.astype(jnp.int32).astype(jnp.float32)
        rows = codes.shape[0] - HEAD
        head = [numbers[rows + i : rows + i + 1] for i in range(4)]
        return joined(*head[:2]) + numbers[:rows] * (joined(*head[2:]) * (1.0 / CODE_MAX))

    def x_copy(c, dx):
        return pltpu.make_async_remote_copy(
            src_ref=xsend.at[c, dx - 1],
            dst_ref=xgot.at[c, RING - 1 - dx],
            send_sem=xsend_sem.at[c],
            recv_sem=xrecv_sem.at[c],
            device_id=x_peer(dx),
            device_id_type=MESH,
        )

    def x_all(c):
        return pltpu.make_async_remote_copy(
            src_ref=xsend.at[c],
            dst_ref=xgot.at[c],
            send_sem=xsend_sem.at[c],
            recv_sem=xrecv_sem.at[c],
            device_id=x_peer(1),
            device_id_type=MESH,
        )

    def send_x(c):
        for dx in (2, 1, 3):
            xsend[c, dx - 1] = encode(acc[c, lax.rem(x + dx, RING)])
            x_copy(c, dx).start()

    def z_copy(c):
        return pltpu.make_async_remote_copy(
            src_ref=zsend.at[c],
            dst_ref=zgot.at[c],
            send_sem=hsend_sem.at[c],
            recv_sem=hrecv_sem.at[c],
            device_id=across,
            device_id_type=MESH,
        )

    def sum_x(c):
        x_all(c).wait_recv()
        total = acc[c, x] + decode(xgot[c, 0]) + decode(xgot[c, 1]) + decode(xgot[c, 2])
        early, late = total[: LANES // 2], total[LANES // 2 :]
        share0 = jnp.where(lane < SHARE, early, pltpu.roll(late, SHARE, 1))
        share1 = jnp.where(lane < SHARE, pltpu.roll(early, SHARE, 1), late)
        first = z_hi == 0
        zsend[c] = encode(jnp.where(first, share1, share0))
        z_copy(c).start()
        own[c] = jnp.where(first, share0, share1)

    def integrate(c):
        z_copy(c).wait_recv()
        total = own[c] + decode(zgot[c])
        turned = pltpu.roll(total, SHARE, 1)
        mine = pl.ds(pl.multiple_of(c * GROUP, GROUP), GROUP)
        membrane = pot_ref[mine, :]
        leak, drive = leak_ref[...], drive_ref[...]
        for s in range(STEPS):
            half = total if s < STEPS // 2 else turned
            begin = s % (STEPS // 2) * GROUP
            synaptic = half[begin : begin + GROUP, :SHARE]
            membrane = membrane + leak * (drive - membrane + synaptic)
            rates_ref[s, mine, :] = jnp.maximum(membrane, 0.0) + jnp.log1p(jnp.exp(-jnp.abs(membrane)))
        last_ref[mine, :] = membrane

    loads[2].wait()

    def slot(k, _):
        def one(c, _):
            t = k - OFFSET * c

            @pl.when(jnp.logical_and(t >= 0, t < CHAIN))
            def _():
                spread(c, t)

            return 0

        def two(c, _):
            t = k - OFFSET * c - LAG

            @pl.when(jnp.logical_and(t == 0, c == 0))
            def _():
                for load in loads[3:]:
                    load.wait()

            @pl.when(jnp.logical_and(t >= 0, t < CHAIN))
            def _():
                product(c, t)

            @pl.when(t == CHAIN - 1)
            def _():
                send_x(c)

            return 0

        lax.fori_loop(0, PASSES, one, 0)
        lax.fori_loop(0, PASSES, two, 0)
        return 0

    lax.fori_loop(0, OFFSET * (PASSES - 1) + CHAIN + LAG, slot, 0)

    def drain(n, _):
        c, t = n // CHAIN, lax.rem(n, CHAIN)
        zs = source_of(t)

        @pl.when(goes_right(zs))
        def _():
            chain_copy(c, t, zs, True).wait_send()

        @pl.when(goes_left(zs))
        def _():
            chain_copy(c, t, zs, False).wait_send()

        windows_copy(c, t).wait_send()
        return 0

    for c in range(PASSES):
        sum_x(c)
    lax.fori_loop(0, PASSES * CHAIN, drain, 0)
    for c in range(PASSES):
        integrate(c)
    for c in range(PASSES):
        x_all(c).wait_send()
        z_copy(c).wait_send()


def on_device(history, weights, delays, area_blocks, potential, leak, drive):
    vmem = pl.BlockSpec(memory_space=pltpu.VMEM)
    dma = pltpu.SemaphoreType.DMA
    bf16, f32 = jnp.bfloat16, jnp.float32
    return pl.pallas_call(
        kernel,
        out_shape=(
            pltpu.VMEM((STEPS, TRIALS, SHARE), f32),
            pltpu.VMEM((TRIALS, SHARE), f32),
        ),
        in_specs=[pl.BlockSpec(memory_space=pltpu.HBM)] * 7,
        out_specs=(vmem, vmem),
        scratch_shapes=[
            pltpu.VMEM(history.shape, f32),
            pltpu.VMEM(weights.shape, bf16),
            pltpu.SMEM(delays.shape, jnp.int32),
            pltpu.SMEM(area_blocks.shape, jnp.int32),
            pltpu.VMEM(potential.shape, f32),
            pltpu.VMEM((1, SHARE), f32),
            pltpu.VMEM((1, SHARE), f32),
            pltpu.VMEM((PASSES, CHAIN, SPANS, SHARE, LANES), bf16),
            pltpu.VMEM((SPANS, SHARE, LANES), SPAN_TYPE),
            pltpu.VMEM((PASSES, CHAIN, PEERS - 1, SHARE, LANES), bf16),
            pltpu.VMEM((PASSES, CHAIN, PEERS, SHARE, LANES), bf16),
            pltpu.VMEM((PASSES, RING, LANES, 2 * SHARE), f32),
            pltpu.VMEM((PASSES, LANES // 2, 2 * SHARE), f32),
            pltpu.VMEM((PASSES, RING - 1, LANES + HEAD, 2 * SHARE), jnp.int16),
            pltpu.VMEM((PASSES, RING - 1, LANES + HEAD, 2 * SHARE), jnp.int16),
            pltpu.VMEM((PASSES, LANES // 2 + HEAD, 2 * SHARE), jnp.int16),
            pltpu.VMEM((PASSES, LANES // 2 + HEAD, 2 * SHARE), jnp.int16),
            pltpu.SMEM((CHAIN,), jnp.int32),
            pltpu.SMEM((PEERS,), jnp.int32),
            dma((7,)),
            dma((2, PASSES, CHAIN)),
            dma((PASSES, CHAIN)),
            dma((PASSES, CHAIN)),
            dma((PASSES, CHAIN)),
            dma((PASSES,)),
            dma((PASSES,)),
            dma((PASSES,)),
            dma((PASSES,)),
        ],
        compiler_params=pltpu.CompilerParams(
            collective_id=0, has_side_effects=True, vmem_limit_bytes=56 * 2**20
        ),
        name="network_interval",
    )(history, weights, delays, area_blocks, potential, leak.reshape(1, -1), drive.reshape(1, -1))


def solution(mesh):
    in_specs = (
        P(("blk", "tgt"), None),
        P(None, "tgt", "blk"),
        P(),
        P(),
        P(None, ("blk", "tgt")),
        P(("blk", "tgt")),
        P(("blk", "tgt")),
    )
    out_specs = (P(None, None, ("blk", "tgt")), P(None, ("blk", "tgt")))
    return jax.shard_map(
        on_device, mesh=mesh, in_specs=in_specs, out_specs=out_specs, check_vma=False
    )
```
